512 devices in a mesh: row: 32 (over z, core), col: 16 (over y, x).
Axes of the slice: x: 4, y: 4, z: 16, core: 2. Of those that a mesh axis runs over, the one named last changes fastest.
Arguments:
- example_sketch: float32 [512, 32768], P('col', 'row'), may hold values from -6 to 6
- candidate_sketch: float32 [512, 32768], P('row', 'col'), may hold values from -6 to 6
- best_start: float32 [32768], P('row'), may hold values from -1 to 1.5
- chosen: int32 [2], replicated, may hold values from 0 to 32767
Outputs:
- best: float32 [32768], P('row')
- gains: float32 [2, 32768], P(None, 'col')
The draws below stay inside these ranges and needn't reach their ends.
All inputs are finite; a program needn't handle non-finite values.
Results may differ from the reference program's by a relative error of at most 0.000075.
Values sent between devices are 32-bit elements; how exact they have to be, the bound alone decides.
A program may use at most 64 MiB of HBM per device.

```python
import jax
import jax.numpy as jnp
from jax import lax

W = 512
C_DEV = 2048
ROUNDS = 2
EXAMPLES = 32768
CANDIDATES = 32768


def level_of(key, shape, cuts, least, largest):
    level = 1.0
    for axis_at, shards_of in cuts:
        draws = jax.random.uniform(jax.random.fold_in(jax.random.fold_in(key, 6), axis_at), (shards_of,), jnp.float32, least / len(cuts), largest / len(cuts))
        level = level * jnp.repeat(jnp.exp(draws), shape[axis_at] // shards_of).reshape((-1,) + (1,) * (len(shape) - 1 - axis_at))
    return level


def scatter_about(key, shape, scale, limit, shards=(), dtype=jnp.bfloat16):
    array = jax.random.normal(key, shape, jnp.float32) * scale
    if len(shards) > 0:
        array = level_of(key, shape, shards, -0.22, 0.18) * array
    return jnp.clip(array, min=-limit, max=limit).astype(dtype)


def setup_inputs(seed: int = 0) -> dict:
    key_list = jax.random.split(jax.random.key(seed), 5)
    example_sketch = scatter_about(key_list[0], (W, EXAMPLES), 1.0, 6.0, ((0, 16), (1, 32)), jnp.float32)
    candidate_sketch = scatter_about(key_list[1], (W, CANDIDATES), 1.0, 6.0, ((0, 32), (1, 16)), jnp.float32)
    best_start = jnp.clip(-1.0 + 2.5 * jax.random.uniform(key_list[2], (EXAMPLES,), jnp.float32) ** level_of(key_list[2], (EXAMPLES,), ((0, 32),), -0.2, 0.2), -1.0, 1.5)
    chosen = jax.random.randint(key_list[3], (ROUNDS,), 0, CANDIDATES).astype(jnp.int32)
    return dict(example_sketch=example_sketch, candidate_sketch=candidate_sketch, best_start=best_start, chosen=chosen)


EPS = 1e-06

def reference(example_sketch, candidate_sketch, best_start, chosen):
    scale = jnp.sqrt(jnp.float32(W))
    ex_norm = jnp.sqrt(lax.optimization_barrier(jnp.sum(example_sketch * example_sketch, axis=0)) + EPS)
    cand_norm = jnp.sqrt(lax.optimization_barrier(jnp.sum(candidate_sketch * candidate_sketch, axis=0)) + EPS)
    factor = scale / ex_norm
    picked = jnp.take(candidate_sketch, chosen, axis=1)
    picked_norm = jnp.take(cand_norm, chosen, axis=0)
    columns = jnp.dot(example_sketch.T, picked, precision=lax.Precision.HIGHEST, preferred_element_type=jnp.float32)
    columns = columns * factor[:, None] / picked_norm[None, :]
    bests = []
    best = best_start
    for step in range(ROUNDS):
        best = jnp.maximum(best, columns[:, step])
        bests.append(best)
    stacked = jnp.stack(bests)
    blocks = jnp.transpose(candidate_sketch.reshape(W, CANDIDATES // C_DEV, C_DEV), (1, 0, 2))
    block_norms = cand_norm.reshape(CANDIDATES // C_DEV, C_DEV)

    def one_block(pair):
        sketch, norms = pair
        similar = jnp.dot(example_sketch.T, sketch, precision=lax.Precision.HIGHEST, preferred_element_type=jnp.float32)
        similar = similar * factor[:, None] / norms[None, :]
        rows = [lax.optimization_barrier(jnp.sum(jnp.maximum(similar - stacked[step][:, None], 0.0), axis=0)) for step in range(ROUNDS)]
        return jnp.stack(rows)
    result = lax.map(one_block, (blocks, block_norms))
    gains = jnp.transpose(result, (1, 0, 2)).reshape(ROUNDS, CANDIDATES) / EXAMPLES
    return (best, gains)
```

```python
import functools

import jax
import jax.numpy as jnp
from jax import lax
from jax.experimental import pallas as pl
from jax.experimental.pallas import tpu as pltpu
from jax.sharding import PartitionSpec as P

EPS = 1e-06
LEVELS = 16
GROUP = 32
PIECES = 4
TILE = 256
F32, BF16 = jnp.float32, jnp.bfloat16


def remote(src, dst, send, recv, row, col):
    return pltpu.make_async_remote_copy(
        src_ref=src,
        dst_ref=dst,
        send_sem=send,
        recv_sem=recv,
        device_id={"row": row, "col": col},
        device_id_type=pl.DeviceIdType.MESH,
    )


def slot_rows(slot):
    return pl.ds((slot % LEVELS) * GROUP, GROUP)


def kernel(
    ex_hbm, cand_hbm, best_ref, chosen_ref, best_out, gains_out,
    cand, c_hi, c_lo, c_sq, ex, e_hi, e_lo, acc, best_rep, ch_part, ch, ch_hi, ch_lo,
    g_own, g_sib, g_all, g_sum,
    loc_sem, ring_s, ring_r, sib_s, sib_r, p1_s, p1_r, p2_s, p2_r,
    cx_s, cx_r, z1_s, z1_r, z2_s, z2_r, gs_s, gs_r, gz_s, gz_r, gf_s, gf_r,
):
    row, col = lax.axis_index("row"), lax.axis_index("col")
    z, c, y, x = row // 2, row % 2, col // 4, col % 4
    xs = [y * 4 + (x + j) % 4 for j in range(1, 4)]
    ys = [((y + j) % 4) * 4 + x for j in range(1, 4)]
    above, below = ((z + 1) % LEVELS) * 2, ((z + LEVELS - 1) % LEVELS) * 2
    sib = z * 2 + 1 - c
    onward = jnp.where(c == 0, above, below + 1)
    pending = []

    def go(*args):
        copy = remote(*args)
        copy.start()
        pending.append(copy)

    def arrived(view, sem):
        remote(view, view, loc_sem.at[0], sem, sib, col).wait_recv()

    mine = pl.ds(pl.multiple_of(4 * GROUP + c * 16, 16), 16)
    ex_slot = (col - z + 4 + LEVELS) % LEVELS
    copy_c = pltpu.make_async_copy(cand_hbm, cand.at[mine], loc_sem.at[0])
    copy_e = pltpu.make_async_copy(
        ex_hbm, ex.at[pl.ds(pl.multiple_of(ex_slot * GROUP, GROUP), GROUP)], loc_sem.at[1]
    )
    copy_c.start()
    copy_e.start()

    barrier = pltpu.get_barrier_semaphore()
    near = [(r, col) for r in (above, above + 1, below, below + 1, sib)]
    near += [(row, t) for t in xs + ys]
    for r, t in near:
        pl.semaphore_signal(
            barrier, inc=1, device_id={"row": r, "col": t}, device_id_type=pl.DeviceIdType.MESH
        )
    pl.semaphore_wait(barrier, len(near))
    copy_c.wait()

    width = cand.shape[1] * 2 // PIECES

    def piece(first_row, half, k):
        start = pl.multiple_of(first_row + 8 * half, 8)
        return cand.at[pl.ds(start, 8), pl.ds((k // 2) * width, width)]

    for k in range(PIECES):
        src = piece(4 * GROUP + c * 16, k % 2, k)
        go(src, piece(3 * GROUP + c * 16, k % 2, k), ring_s.at[0, 0, k], ring_r.at[0, c, k], above, col)
        go(src, piece(5 * GROUP + c * 16, k % 2, k), ring_s.at[0, 1, k], ring_r.at[0, c, k], below + 1, col)
    go(cand.at[mine], cand.at[mine], sib_s.at[0], sib_r.at[0], sib, col)

    copy_e.wait()

    def ex_view(t, half):
        slot = (t - z + 4 + LEVELS) % LEVELS
        return ex.at[pl.ds(pl.multiple_of(slot * GROUP + 16 * half, 16), 16)]

    for j in range(3):
        go(ex_view(col, 0), ex_view(col, 0), p1_s.at[0, j], p1_r.at[0, j], row, xs[j])
        go(ex_view(col, 1), ex_view(col, 1), p1_s.at[1, j], p1_r.at[1, j], row, ys[j])
    for j in range(3):
        go(ex_view(col, 0), ex_view(col, 0), p2_s.at[0, 3, j], p2_r.at[0, 3, j], row, ys[j])
        go(ex_view(col, 1), ex_view(col, 1), p2_s.at[1, 3, j], p2_r.at[1, 3, j], row, xs[j])

    def hop(h):
        base = jnp.where(c == 0, ((4 - h) % LEVELS) * GROUP, ((4 + h) % LEVELS) * GROUP)
        after = jnp.where(c == 0, ((3 - h) % LEVELS) * GROUP, ((5 + h) % LEVELS) * GROUP)
        for k in range(PIECES):
            for o in range(2):
                far = k % 2 == 0
                if h == 8 and not far:
                    continue
                half = (k % 2 + c) % 2
                view = piece(base + o * 16, half, k)
                kk = (k // 2) * 2 + half if h == 1 else k
                arrived(view, ring_r.at[h - 1, o, kk])
                if h < 7 or (far and h < 8):
                    go(view, piece(after + o * 16, half, k), ring_s.at[h, o, k], ring_r.at[h, o, k], onward, col)
        if h < 8:
            view = cand.at[pl.ds(pl.multiple_of(base, GROUP), GROUP)]
            go(view, view, sib_s.at[h], sib_r.at[h], sib, col)
        else:
            for o in range(2):
                view = cand.at[pl.ds(pl.multiple_of(base + o * 16 + 8 * c, 8), 8)]
                go(view, view, sib_s.at[8 + o], sib_r.at[8 + o], sib, col)

    def from_sib(h):
        if h == 0:
            arrived(cand.at[pl.ds(0, 16)], sib_r.at[0])
        elif h < 8:
            arrived(cand.at[pl.ds(0, GROUP)], sib_r.at[h])
        else:
            for o in range(2):
                arrived(cand.at[pl.ds(0, 8)], sib_r.at[8 + o])

    def prepare(slot):
        v = cand[slot_rows(slot), :]
        hi = v.astype(BF16)
        c_hi[slot_rows(slot), :] = hi
        c_lo[slot_rows(slot), :] = (v - hi.astype(F32)).astype(BF16)
        sq = v * v
        c_sq[...] += sq[0:8] + sq[8:16] + sq[16:24] + sq[24:32]

    lane = lax.broadcasted_iota(jnp.int32, (128, 128), 1)
    sub = lax.broadcasted_iota(jnp.int32, (128, 128), 0)

    c_sq[...] = jnp.zeros_like(c_sq)
    for i in range(8):
        best_rep[0, pl.ds(128 * i, 128), :] = jnp.broadcast_to(best_ref[pl.ds(i, 1), :], (128, 128)).T
    from_sib(0)
    level = cand[slot_rows(4), :]
    wide = lax.broadcasted_iota(jnp.int32, level.shape, 1)
    tile = jnp.zeros((8, 128), F32)
    for r in range(2):
        at = chosen_ref[r] - col * level.shape[1]
        value = jnp.sum(jnp.where(wide == at, level, 0.0), axis=1, keepdims=True)
        line = jnp.sum(
            jnp.where(lane[:GROUP] == sub[:GROUP] + GROUP * (z % 4), value, 0.0), axis=0, keepdims=True
        )
        tile = tile + jnp.where(sub[:8] == r, line, 0.0)
    ch_part[0] = tile
    for j in range(3):
        go(ch_part.at[0], ch_part.at[2 + j], cx_s.at[0, j], cx_r.at[0, j], row, xs[j])
    prepare(4)

    hop(1)
    for i in (0, 2, 1):
        bx, by = y * 4 + (x + 3 - i) % 4, ((y + 3 - i) % 4) * 4 + x
        arrived(ex_view(bx, 0), p1_r.at[0, i])
        for j in range(3):
            go(ex_view(bx, 0), ex_view(bx, 0), p2_s.at[0, i, j], p2_r.at[0, i, j], row, ys[j])
        arrived(ex_view(by, 1), p1_r.at[1, i])
        for j in range(3):
            go(ex_view(by, 1), ex_view(by, 1), p2_s.at[1, i, j], p2_r.at[1, i, j], row, xs[j])
    for j in range(3):
        arrived(ch_part.at[2 + j], cx_r.at[0, j])
    ch_part[1] = ch_part[0] + ch_part[2] + ch_part[3] + ch_part[4]
    for j in range(3):
        go(ch_part.at[1], ch_part.at[5 + j], cx_s.at[1, j], cx_r.at[1, j], row, ys[j])
    from_sib(1)
    prepare(3)
    prepare(5)

    hop(2)
    for j in range(3):
        arrived(ch_part.at[5 + j], cx_r.at[1, j])
    ch[4] = ch_part[1] + ch_part[5] + ch_part[6] + ch_part[7]
    from_sib(2)
    prepare(2)
    prepare(6)

    hop(3)
    from_sib(3)
    prepare(1)
    prepare(7)

    hop(4)
    from_sib(4)
    for d in range(1, 5):
        go(ch.at[4], ch.at[4 - d], z1_s.at[0, d - 1], z1_r.at[0, d - 1], ((z + d) % LEVELS) * 2 + c, col)
        go(ch.at[4], ch.at[4 + d], z1_s.at[1, d - 1], z1_r.at[1, d - 1], ((z + LEVELS - d) % LEVELS) * 2 + c, col)
    prepare(0)
    prepare(8)

    hop(5)
    for half in range(2):
        for i in range(4):
            for j in range(3):
                arrived(ex.at[pl.ds(0, 16)], p2_r.at[half, i, j])
    e_sq = jnp.zeros((8, ex.shape[1]), F32)
    for i in range(64):
        v = ex[pl.ds(8 * i, 8), :]
        e_sq = e_sq + v * v
    factor = jnp.sqrt(jnp.float32(LEVELS * GROUP)) / jnp.sqrt(jnp.sum(e_sq, axis=0, keepdims=True) + EPS)
    from_sib(5)
    for d in range(1, 5):
        arrived(ch.at[0], z1_r.at[0, d - 1])
        arrived(ch.at[0], z1_r.at[1, d - 1])
    go(ch.at[pl.ds(0, 4)], ch.at[pl.ds(12, 4)], z2_s.at[0], z2_r.at[0], ((z + 4) % LEVELS) * 2 + c, col)
    go(ch.at[pl.ds(5, 3)], ch.at[pl.ds(9, 3)], z2_s.at[1], z2_r.at[1], ((z + LEVELS - 4) % LEVELS) * 2 + c, col)
    prepare(15)
    prepare(9)

    hop(6)
    for i in range(8):
        for q in range(4):
            block = ex[pl.ds(128 * q, 128), pl.ds(128 * i, 128)] * factor[:, 128 * i : 128 * (i + 1)]
            block = block.T
            hi = block.astype(BF16)
            e_hi[pl.ds(128 * i, 128), pl.ds(128 * q, 128)] = hi
            e_lo[pl.ds(128 * i, 128), pl.ds(128 * q, 128)] = (block - hi.astype(F32)).astype(BF16)
    from_sib(6)
    prepare(14)
    prepare(10)

    def product(first, hi, lo):
        a_hi, a_lo = e_hi[:, pl.ds(first, 256)], e_lo[:, pl.ds(first, 256)]
        dot = functools.partial(jnp.dot, preferred_element_type=F32)
        return dot(a_hi, hi) + dot(a_lo, hi) + dot(a_hi, lo)

    hop(7)
    arrived(ch.at[pl.ds(0, 4)], z2_r.at[0])
    arrived(ch.at[pl.ds(0, 3)], z2_r.at[1])
    ch_sq = [jnp.zeros((1, 128), F32), jnp.zeros((1, 128), F32)]
    for q in range(4):
        four = ch[4 * q] + ch[4 * q + 1] + ch[4 * q + 2] + ch[4 * q + 3]
        for r in range(2):
            v = jnp.broadcast_to(four[r : r + 1, :], (128, 128)).T
            ch_sq[r] = ch_sq[r] + jnp.sum(v * v, axis=0, keepdims=True)
            hi = v.astype(BF16)
            lo = (v - hi.astype(F32)).astype(BF16)
            for b in range(4):
                to = pl.ds(pl.multiple_of(((b - z + LEVELS) % 4 + 4 * q) * GROUP, GROUP), GROUP)
                ch_hi[to, pl.ds(128 * r, 128)] = hi[32 * b : 32 * b + 32]
                ch_lo[to, pl.ds(128 * r, 128)] = lo[32 * b : 32 * b + 32]

    def pick(i, _):
        rows = pl.ds(pl.multiple_of(i * 128, 128), 128)
        dot = functools.partial(jnp.dot, preferred_element_type=F32)
        hi, lo = e_hi[rows, :], e_lo[rows, :]
        d = dot(hi, ch_hi[...]) + dot(lo, ch_hi[...]) + dot(hi, ch_lo[...])
        b = best_rep[0, rows, :]
        for r in range(2):
            b = jnp.maximum(b, d[:, 128 * r : 128 * r + 128] / jnp.sqrt(ch_sq[r] + EPS))
            best_rep[r, rows, :] = b
        best_out[pl.ds(i, 1), :] = jnp.sum(jnp.where(lane == sub, b, 0.0), axis=0, keepdims=True)
        return 0

    lax.fori_loop(0, 8, pick, 0)

    def first_half(n, _):
        cols = pl.ds(pl.multiple_of(n * TILE, TILE), TILE)
        acc[:, cols] = product(0, c_hi[pl.ds(0, 256), cols], c_lo[pl.ds(0, 256), cols])
        return 0

    lax.fori_loop(0, 8, first_half, 0)
    from_sib(7)
    prepare(13)
    prepare(11)

    hop(8)
    from_sib(8)
    prepare(12)

    def second_half(n, _):
        cols = pl.ds(pl.multiple_of(n * TILE, TILE), TILE)
        d = acc[:, cols] + product(256, c_hi[pl.ds(256, 256), cols], c_lo[pl.ds(256, 256), cols])
        norm = jnp.sqrt(jnp.sum(c_sq[:, cols], axis=0, keepdims=True) + EPS)
        sim = d * (1.0 / norm)
        for r in range(2):
            b = best_rep[r]
            for t in range(2):
                part = jnp.maximum(sim[:, 128 * t : 128 * t + 128] - b, 0.0)
                g_own[r, pl.ds(2 * n + t, 1), :] = jnp.sum(part, axis=0, keepdims=True)
        return 0

    def to_sib(p):
        go(g_own.at[1 - c, pl.ds(8 * p, 8)], g_sib.at[pl.ds(8 * p, 8)], gs_s.at[p], gs_r.at[p], sib, col)

    def to_levels(p):
        part = pl.ds(8 * p, 8)
        arrived(g_sib.at[part], gs_r.at[p])
        g_all[0, part] = g_own[c, part] + g_sib[part]
        for d in (8, 7, 9, 6, 10, 5, 11, 4, 12, 3, 13, 2, 14, 1, 15):
            go(g_all.at[0, part], g_all.at[d, part], gz_s.at[p, d - 1], gz_r.at[p, d - 1],
               ((z + d) % LEVELS) * 2 + c, col)

    lax.fori_loop(0, 4, second_half, 0)
    to_sib(0)
    lax.fori_loop(4, 6, second_half, 0)
    to_levels(0)
    lax.fori_loop(6, 8, second_half, 0)
    to_sib(1)
    to_levels(1)
    for p in range(2):
        part = pl.ds(8 * p, 8)
        for d in range(1, LEVELS):
            arrived(g_all.at[d, part], gz_r.at[p, d - 1])
    total = g_all[0]
    for d in range(1, LEVELS):
        total = total + g_all[d]
    g_sum[c] = total * (1.0 / 32768.0)
    go(g_sum.at[c], g_sum.at[c], gf_s, gf_r, sib, col)
    arrived(g_sum.at[1 - c], gf_r)
    for r in range(2):
        for t in range(16):
            gains_out[pl.ds(r, 1), pl.ds(128 * t, 128)] = g_sum[r, pl.ds(t, 1), :]
    for copy in pending:
        copy.wait_send()


def on_device(example_sketch, candidate_sketch, best_start, chosen):
    dma = pltpu.SemaphoreType.DMA
    vmem = pltpu.VMEM
    examples, candidates = example_sketch.shape[1], candidate_sketch.shape[1]
    widths = LEVELS * GROUP
    best, gains = pl.pallas_call(
        kernel,
        out_shape=(
            jax.ShapeDtypeStruct((8, 128), F32),
            jax.ShapeDtypeStruct((2, candidates), F32),
        ),
        in_specs=[
            pl.BlockSpec(memory_space=pl.ANY),
            pl.BlockSpec(memory_space=pl.ANY),
            pl.BlockSpec(memory_space=pltpu.VMEM),
            pl.BlockSpec(memory_space=pltpu.SMEM),
        ],
        out_specs=(pl.BlockSpec(memory_space=pltpu.VMEM), pl.BlockSpec(memory_space=pltpu.VMEM)),
        scratch_shapes=[
            vmem((widths, candidates), F32),
            vmem((widths, candidates), BF16),
            vmem((widths, candidates), BF16),
            vmem((8, candidates), F32),
            vmem((widths, examples), F32),
            vmem((examples, widths), BF16),
            vmem((examples, widths), BF16),
            vmem((examples, candidates), F32),
            vmem((2, examples, 128), F32),
            vmem((8, 8, 128), F32),
            vmem((LEVELS, 8, 128), F32),
            vmem((widths, 256), BF16),
            vmem((widths, 256), BF16),
            vmem((2, 16, 128), F32),
            vmem((16, 128), F32),
            vmem((LEVELS, 16, 128), F32),
            vmem((2, 16, 128), F32),
            dma((2,)),
            dma((8, 2, PIECES)),
            dma((8, 2, PIECES)),
            dma((10,)),
            dma((10,)),
            dma((2, 3)),
            dma((2, 3)),
            dma((2, 4, 3)),
            dma((2, 4, 3)),
            dma((2, 3)),
            dma((2, 3)),
            dma((2, 4)),
            dma((2, 4)),
            dma((2,)),
            dma((2,)),
            dma((2,)),
            dma((2,)),
            dma((2, 15)),
            dma((2, 15)),
            dma,
            dma,
        ],
        compiler_params=pltpu.CompilerParams(
            collective_id=0, has_side_effects=True, vmem_limit_bytes=48 * 1024 * 1024
        ),
        cost_estimate=pl.CostEstimate(flops=6 * 512 * 1024 * 2048, bytes_accessed=300000, transcendentals=4096),
    )(example_sketch, candidate_sketch, best_start.reshape(8, 128), chosen)
    return best.reshape(examples), gains


def solution(mesh):
    return jax.shard_map(
        on_device,
        mesh=mesh,
        in_specs=(P("col", "row"), P("row", "col"), P("row"), P()),
        out_specs=(P("row"), P(None, "col")),
        check_vma=False,
    )
```

```python
import functools

import jax
import jax.numpy as jnp
from jax import lax
from jax.experimental import pallas as pl
from jax.experimental.pallas import tpu as pltpu
from jax.sharding import PartitionSpec as P

EPS = 1e-06
LEVELS = 16
GROUP = 32
PIECES = 4
TILE = 256
F32, BF16 = jnp.float32, jnp.bfloat16


def remote(src, dst, send, recv, row, col):
    return pltpu.make_async_remote_copy(
        src_ref=src,
        dst_ref=dst,
        send_sem=send,
        recv_sem=recv,
        device_id={"row": row, "col": col},
        device_id_type=pl.DeviceIdType.MESH,
    )


def slot_rows(slot):
    return pl.ds((slot % LEVELS) * GROUP, GROUP)


def kernel(
    ex_hbm, cand_hbm, best_hbm, chosen_hbm, best_out, gains_out,
    cand, c_hi, c_lo, c_sq, ex, e_hi, e_lo, acc, best_rep, best_in, chosen, ch_part, ch, ch_hi, ch_lo,
    g_own, g_sib, g_all, g_sum,
    loc_sem, ring_s, ring_r, sib_s, sib_r, p1_s, p1_r, p2_s, p2_r, wave,
    cx_s, cx_r, z1_s, z1_r, z2_s, z2_r, gs_s, gs_r, gz_s, gz_r, gf_s, gf_r,
):
    row, col = lax.axis_index("row"), lax.axis_index("col")
    z, c, y, x = row // 2, row % 2, col // 4, col % 4

    def in_x(d):
        return y * 4 + (x + d) % 4

    def in_y(d):
        return ((y + d) % 4) * 4 + x

    def in_z(d):
        return ((z + d + LEVELS) % LEVELS) * 2 + c

    above, below = ((z + 1) % LEVELS) * 2, ((z + LEVELS - 1) % LEVELS) * 2
    sib = z * 2 + 1 - c
    onward = jnp.where(c == 0, above, below + 1)
    pending = []

    def go(*args):
        copy = remote(*args)
        copy.start()
        pending.append(copy)

    def arrived(view, sem):
        remote(view, view, loc_sem.at[0], sem, sib, col).wait_recv()

    barrier = pltpu.get_barrier_semaphore()
    near = [(r, col) for r in (above, above + 1, below, below + 1, sib)]
    near += [(row, t) for d in (1, 2, 3) for t in (in_x(d), in_y(d))]
    for r, t in near:
        pl.semaphore_signal(
            barrier, inc=1, device_id={"row": r, "col": t}, device_id_type=pl.DeviceIdType.MESH
        )

    mine = pl.ds(pl.multiple_of(4 * GROUP + c * 16, 16), 16)

    def ex_view(t, half, rows=16, skip=0):
        slot = (t - z + 4 + LEVELS) % LEVELS
        return ex.at[pl.ds(pl.multiple_of(slot * GROUP + 16 * half + skip, 8), rows)]

    copies = [
        pltpu.make_async_copy(cand_hbm, cand.at[mine], loc_sem.at[0]),
        pltpu.make_async_copy(chosen_hbm, chosen, loc_sem.at[1]),
        pltpu.make_async_copy(ex_hbm, ex_view(col, 0, 32), loc_sem.at[2]),
        pltpu.make_async_copy(best_hbm, best_in, loc_sem.at[3]),
    ]
    for copy in copies:
        copy.start()
    copies[0].wait()
    copies[1].wait()

    lane = lax.broadcasted_iota(jnp.int32, (128, 128), 1)
    sub = lax.broadcasted_iota(jnp.int32, (128, 128), 0)

    block = cand[mine, :]
    wide = lax.broadcasted_iota(jnp.int32, block.shape, 1)
    tile = jnp.zeros((8, 128), F32)
    for r in range(2):
        place = chosen[r] - col * block.shape[1]
        value = jnp.sum(jnp.where(wide == place, block, 0.0), axis=1, keepdims=True)
        line = jnp.sum(
            jnp.where(lane[:16] == sub[:16] + (GROUP * (z % 4) + 16 * c), value, 0.0), axis=0, keepdims=True
        )
        tile = tile + jnp.where(sub[:8] == r, line, 0.0)
    ch_part[0] = tile
    copies[2].wait()
    copies[3].wait()
    pl.semaphore_wait(barrier, len(near))

    def wave_send(i):
        for k, r in enumerate((in_z(1), in_z(-1))):
            pl.semaphore_signal(
                wave.at[i, k], inc=1, device_id={"row": r, "col": col}, device_id_type=pl.DeviceIdType.MESH
            )

    def wave_wait(i):
        pl.semaphore_wait(wave.at[i, 0], 1)
        pl.semaphore_wait(wave.at[i, 1], 1)

    wave_send(0)

    width = cand.shape[1] * 2 // PIECES

    def piece(first_row, half, k):
        start = pl.multiple_of(first_row + 8 * half, 8)
        return cand.at[pl.ds(start, 8), pl.ds((k // 2) * width, width)]

    for k in range(PIECES):
        src = piece(4 * GROUP + c * 16, k % 2, k)
        go(src, piece(3 * GROUP + c * 16, k % 2, k), ring_s.at[0, 0, k], ring_r.at[0, c, k], above, col)
        go(src, piece(5 * GROUP + c * 16, k % 2, k), ring_s.at[0, 1, k], ring_r.at[0, c, k], below + 1, col)
    go(cand.at[mine], cand.at[mine], sib_s.at[0, 0, 0], sib_r.at[0], sib, col)
    two = pl.ds(0, 2)
    for j in range(3):
        go(ch_part.at[0, two], ch_part.at[2 + j, two], cx_s.at[0, j], cx_r.at[0, j], row, in_x(j + 1))

    lines = ((in_x, in_y), (in_y, in_x))

    def spread(half, phase, i, view):
        s, r = (p1_s, p1_r) if phase == 0 else (p2_s, p2_r)
        for k, d in enumerate((1, 3)):
            go(view, view, s.at[half, i, k], r.at[half, i, k], row, lines[half][phase](d))

    def relay(half, phase, i, k, owner):
        s, r = (p1_s, p1_r) if phase == 0 else (p2_s, p2_r)
        arrived(ex_view(owner, half), r.at[half, i, k])
        view = ex_view(owner, half, 8, 8 * k)
        go(view, view, s.at[half, i, 2 + k], r.at[half, i, 2 + k], row, lines[half][phase]((1, 3)[k]))

    def opposite(half, phase, i):
        r = p1_r if phase == 0 else p2_r
        arrived(ex.at[pl.ds(0, 8)], r.at[half, i, 2])
        arrived(ex.at[pl.ds(0, 8)], r.at[half, i, 3])

    def first(half, d):
        return lines[half][0](d)

    def second(half, d1, d2):
        xx, yy = (d1, d2) if half == 0 else (d2, d1)
        return ((y + yy) % 4) * 4 + (x + xx) % 4

    for half in range(2):
        spread(half, 0, 0, ex_view(col, half))
    for half in range(2):
        spread(half, 1, 0, ex_view(col, half))

    plan = {}

    def at(h, i, *fns):
        plan.setdefault((h, i), []).extend(fns)

    def call(fn, *args):
        return functools.partial(fn, *args)

    def phase_one(half, k):
        d = (3, 1)[k]
        relay(half, 0, 0, k, first(half, d))
        spread(half, 1, d, ex_view(first(half, d), half))

    def phase_one_far(half):
        opposite(half, 0, 0)
        spread(half, 1, 2, ex_view(first(half, 2), half))

    def phase_two(half, d, k):
        relay(half, 1, d, k, second(half, d, (3, 1)[k]))

    def from_sib(h):
        arrived(cand.at[pl.ds(0, 16 if h in (0, 8) else GROUP)], sib_r.at[h])

    def prepare(slot):
        v = cand[slot_rows(slot), :]
        hi = v.astype(BF16)
        c_hi[slot_rows(slot), :] = hi
        c_lo[slot_rows(slot), :] = (v - hi.astype(F32)).astype(BF16)
        sq = v * v
        c_sq[...] += sq[0:8] + sq[8:16] + sq[16:24] + sq[24:32]

    def chosen_y():
        for j in range(3):
            arrived(ch_part.at[2 + j, two], cx_r.at[0, j])
        ch_part[1, two] = ch_part[0, two] + ch_part[2, two] + ch_part[3, two] + ch_part[4, two]
        for j in range(3):
            go(ch_part.at[1, two], ch_part.at[5 + j, two], cx_s.at[1, j], cx_r.at[1, j], row, in_y(j + 1))

    def chosen_sib():
        for j in range(3):
            arrived(ch_part.at[5 + j, two], cx_r.at[1, j])
        ch_part[8, two] = ch_part[1, two] + ch_part[5, two] + ch_part[6, two] + ch_part[7, two]
        go(ch_part.at[8, two], ch_part.at[9, two], cx_s.at[2, 0], cx_r.at[2, 0], sib, col)

    def chosen_near():
        arrived(ch_part.at[9, two], cx_r.at[2, 0])
        ch[4, two] = ch_part[8, two] + ch_part[9, two]
        for d in range(1, 5):
            go(ch.at[4, two], ch.at[4 - d, two], z1_s.at[0, d - 1], z1_r.at[0, d - 1], in_z(d), col)
            go(ch.at[4, two], ch.at[4 + d, two], z1_s.at[1, d - 1], z1_r.at[1, d - 1], in_z(-d), col)

    def chosen_far():
        for d in range(1, 5):
            arrived(ch.at[0, two], z1_r.at[0, d - 1])
            arrived(ch.at[0, two], z1_r.at[1, d - 1])
        go(ch.at[pl.ds(0, 4), two], ch.at[pl.ds(12, 4), two], z2_s.at[0], z2_r.at[0], in_z(4), col)
        go(ch.at[pl.ds(5, 3), two], ch.at[pl.ds(9, 3), two], z2_s.at[1], z2_r.at[1], in_z(-4), col)

    held = {"e_sq": jnp.zeros((8, ex.shape[1]), F32), "ch_sq": [jnp.zeros((1, 128), F32)] * 2}

    def square(part):
        total = held["e_sq"]
        for i in range(32 * part, 32 * part + 32):
            v = ex[pl.ds(8 * i, 8), :]
            total = total + v * v
        held["e_sq"] = total
        if part == 1:
            scale = jnp.sqrt(jnp.float32(LEVELS * GROUP))
            held["factor"] = scale / jnp.sqrt(jnp.sum(total, axis=0, keepdims=True) + EPS)

    def turn(i, q):
        v = ex[pl.ds(128 * q, 128), pl.ds(128 * i, 128)] * held["factor"][:, 128 * i : 128 * (i + 1)]
        v = v.T
        hi = v.astype(BF16)
        e_hi[pl.ds(128 * i, 128), pl.ds(128 * q, 128)] = hi
        e_lo[pl.ds(128 * i, 128), pl.ds(128 * q, 128)] = (v - hi.astype(F32)).astype(BF16)

    def chosen_wide(q):
        four = ch[4 * q, two] + ch[4 * q + 1, two] + ch[4 * q + 2, two] + ch[4 * q + 3, two]
        for r in range(2):
            v = jnp.broadcast_to(four[r : r + 1, :], (128, 128)).T
            held["ch_sq"] = [
                s + jnp.sum(v * v, axis=0, keepdims=True) if k == r else s for k, s in enumerate(held["ch_sq"])
            ]
            hi = v.astype(BF16)
            lo = (v - hi.astype(F32)).astype(BF16)
            for b in range(4):
                to = pl.ds(pl.multiple_of(((b - z + LEVELS) % 4 + 4 * q) * GROUP, GROUP), GROUP)
                ch_hi[to, pl.ds(128 * r, 128)] = hi[32 * b : 32 * b + 32]
                ch_lo[to, pl.ds(128 * r, 128)] = lo[32 * b : 32 * b + 32]

    def chosen_come():
        arrived(ch.at[pl.ds(0, 4), two], z2_r.at[0])
        arrived(ch.at[pl.ds(0, 3), two], z2_r.at[1])

    dot = functools.partial(jnp.dot, preferred_element_type=F32)

    def pick(i):
        rows = pl.ds(i * 256, 256)
        hi, lo = e_hi[rows, :], e_lo[rows, :]
        d = dot(hi, ch_hi[...]) + dot(lo, ch_hi[...]) + dot(hi, ch_lo[...])
        b = best_rep[0, rows, :]
        for r in range(2):
            b = jnp.maximum(b, d[:, 128 * r : 128 * r + 128] / jnp.sqrt(held["ch_sq"][r] + EPS))
            best_rep[r, rows, :] = b
        for k in range(2):
            best_out[pl.ds(2 * i + k, 1), :] = jnp.sum(
                jnp.where(lane == sub, b[128 * k : 128 * k + 128], 0.0), axis=0, keepdims=True
            )

    def first_half(n, m):
        cols, rows = pl.ds(n * TILE, TILE), pl.ds(m * 512, 512)
        hi, lo = c_hi[pl.ds(0, 256), cols], c_lo[pl.ds(0, 256), cols]
        a_hi, a_lo = e_hi[rows, pl.ds(0, 256)], e_lo[rows, pl.ds(0, 256)]
        acc[rows, cols] = dot(a_hi, hi) + dot(a_lo, hi) + dot(a_hi, lo)

    at(1, 3, call(wave_wait, 2), chosen_y)
    at(2, 7, chosen_sib)
    at(3, 3, chosen_near)
    at(5, 4, chosen_far)
    at(7, 2, chosen_come, call(chosen_wide, 0))
    at(7, 3, call(chosen_wide, 1))
    at(7, 4, call(chosen_wide, 2))
    at(7, 5, call(chosen_wide, 3))
    for n, (half, k) in enumerate(((0, 0), (0, 1), (1, 0), (1, 1))):
        at(1, (1, 2, 4, 5)[n], call(phase_one, half, k))
        at(2, n, call(phase_two, half, 0, k))
        at(3, 2 * (n % 2) + 1, call(phase_two, half, 1, k))
        at(3, 2 * (n % 2) + 4, call(phase_two, half, 3, k))
        at(4, n, call(phase_two, half, 2, k))
    at(2, 5, call(phase_one_far, 0))
    at(2, 6, call(phase_one_far, 1))
    for half in range(2):
        for d in range(4):
            at(5, 0, call(opposite, half, 1, d))
    at(5, 1, call(square, 0))
    at(5, 2, call(square, 1))
    work = [call(turn, i, q) for q in range(2) for i in range(8)]
    for i, fn in enumerate(work):
        at(5, 3 + i // 4, fn)
    work = [call(turn, i, q) for q in range(2, 4) for i in range(8)]
    for i, fn in enumerate(work):
        at(6, 6 + i // 8, fn)
    for h in range(1, 7):
        at(h + 1, 3, call(from_sib, h))
        at(h + 1, 4, call(prepare, (4 - h) % LEVELS))
        at(h + 1, 5, call(prepare, 4 + h))
    halves = [(n, m) for n in range(8) for m in range(2)]
    for i, (n, m) in enumerate(halves[:6]):
        at(6, i, call(first_half, n, m))
    for i, (n, m) in enumerate(halves[6:14]):
        at(7, i, call(first_half, n, m))
    for i, (n, m) in enumerate(halves[14:]):
        at(8, i, call(first_half, n, m))
    for i in range(4):
        at(7, 6 + i // 2, call(pick, i))

    c_sq[...] = jnp.zeros_like(c_sq)
    for i in range(8):
        best_rep[0, pl.ds(128 * i, 128), :] = jnp.broadcast_to(best_in[pl.ds(i, 1), :], (128, 128)).T
    wave_wait(0)
    wave_send(1)
    from_sib(0)
    prepare(4)
    wave_wait(1)
    wave_send(2)

    for h in range(1, 9):
        base = jnp.where(c == 0, ((4 - h) % LEVELS) * GROUP, ((4 + h) % LEVELS) * GROUP)
        after = jnp.where(c == 0, ((3 - h) % LEVELS) * GROUP, ((5 + h) % LEVELS) * GROUP)
        event = 0
        for k in range(PIECES):
            for o in range(2):
                far = k % 2 == 0
                if h == 8 and not far:
                    continue
                half = (k % 2 + c) % 2
                view = piece(base + o * 16, half, k)
                kk = (k // 2) * 2 + half if h == 1 else k
                arrived(view, ring_r.at[h - 1, o, kk])
                if h < 7 or (far and h < 8):
                    go(view, piece(after + o * 16, half, k), ring_s.at[h, o, k], ring_r.at[h, o, k], onward, col)
                go(view, view, sib_s.at[h, o, k], sib_r.at[h], sib, col)
                for fn in plan.pop((h, event), ()):
                    fn()
                event += 1
    assert not plan
    from_sib(7)
    prepare(13)
    prepare(11)
    from_sib(8)
    prepare(12)

    def second_half(n, _):
        cols = pl.ds(pl.multiple_of(n * TILE, TILE), TILE)
        hi, lo = c_hi[pl.ds(256, 256), cols], c_lo[pl.ds(256, 256), cols]
        a_hi, a_lo = e_hi[:, pl.ds(256, 256)], e_lo[:, pl.ds(256, 256)]
        d = acc[:, cols] + (dot(a_hi, hi) + dot(a_lo, hi) + dot(a_hi, lo))
        norm = jnp.sqrt(jnp.sum(c_sq[:, cols], axis=0, keepdims=True) + EPS)
        sim = d * (1.0 / norm)
        for r in range(2):
            b = best_rep[r]
            for t in range(2):
                part = jnp.maximum(sim[:, 128 * t : 128 * t + 128] - b, 0.0)
                g_own[r, pl.ds(2 * n + t, 1), :] = jnp.sum(part, axis=0, keepdims=True)
        return 0

    def rows_of(p):
        return pl.ds(4 * p, 4)

    def to_sib(p):
        go(g_own.at[1 - c, rows_of(p)], g_sib.at[rows_of(p)], gs_s.at[p], gs_r.at[p], sib, col)

    def to_levels(p):
        part = rows_of(p)
        arrived(g_sib.at[part], gs_r.at[p])
        g_all[0, part] = g_own[c, part] + g_sib[part]
        for d in (8, 7, 9, 6, 10, 5, 11, 4, 12, 3, 13, 2, 14, 1, 15):
            go(g_all.at[0, part], g_all.at[d, part], gz_s.at[p, d - 1], gz_r.at[p, d - 1], in_z(d), col)

    for p in range(4):
        lax.fori_loop(2 * p, 2 * p + 2, second_half, 0)
        to_sib(p)
        if p > 0:
            to_levels(p - 1)
    to_levels(3)
    for p in range(4):
        for d in range(1, LEVELS):
            arrived(g_all.at[d, rows_of(p)], gz_r.at[p, d - 1])
    total = g_all[0]
    for d in range(1, LEVELS):
        total = total + g_all[d]
    g_sum[c] = total * (1.0 / 32768.0)
    go(g_sum.at[c], g_sum.at[c], gf_s, gf_r, sib, col)
    arrived(g_sum.at[1 - c], gf_r)
    for r in range(2):
        for t in range(16):
            gains_out[pl.ds(r, 1), pl.ds(128 * t, 128)] = g_sum[r, pl.ds(t, 1), :]
    for copy in pending:
        copy.wait_send()


def on_device(example_sketch, candidate_sketch, best_start, chosen):
    dma = pltpu.SemaphoreType.DMA
    vmem = pltpu.VMEM
    examples, candidates = example_sketch.shape[1], candidate_sketch.shape[1]
    widths = LEVELS * GROUP
    best, gains = pl.pallas_call(
        kernel,
        out_shape=(
            jax.ShapeDtypeStruct((8, 128), F32),
            jax.ShapeDtypeStruct((2, candidates), F32),
        ),
        in_specs=[
            pl.BlockSpec(memory_space=pltpu.HBM),
            pl.BlockSpec(memory_space=pltpu.HBM),
            pl.BlockSpec(memory_space=pltpu.HBM),
            pl.BlockSpec(memory_space=pltpu.HBM),
        ],
        out_specs=(pl.BlockSpec(memory_space=pltpu.VMEM), pl.BlockSpec(memory_space=pltpu.VMEM)),
        scratch_shapes=[
            vmem((widths, candidates), F32),
            vmem((widths, candidates), BF16),
            vmem((widths, candidates), BF16),
            vmem((8, candidates), F32),
            vmem((widths, examples), F32),
            vmem((examples, widths), BF16),
            vmem((examples, widths), BF16),
            vmem((examples, candidates), F32),
            vmem((2, examples, 128), F32),
            vmem((8, 128), F32),
            pltpu.SMEM((2,), jnp.int32),
            vmem((10, 8, 128), F32),
            vmem((LEVELS, 8, 128), F32),
            vmem((widths, 256), BF16),
            vmem((widths, 256), BF16),
            vmem((2, 16, 128), F32),
            vmem((16, 128), F32),
            vmem((LEVELS, 16, 128), F32),
            vmem((2, 16, 128), F32),
            dma((4,)),
            dma((8, 2, PIECES)),
            dma((8, 2, PIECES)),
            dma((9, 2, PIECES)),
            dma((9,)),
            dma((2, 1, 4)),
            dma((2, 1, 4)),
            dma((2, 4, 4)),
            dma((2, 4, 4)),
            pltpu.SemaphoreType.REGULAR((3, 2)),
            dma((3, 3)),
            dma((3, 3)),
            dma((2, 4)),
            dma((2, 4)),
            dma((2,)),
            dma((2,)),
            dma((4,)),
            dma((4,)),
            dma((4, 15)),
            dma((4, 15)),
            dma,
            dma,
        ],
        compiler_params=pltpu.CompilerParams(
            collective_id=0, has_side_effects=True, vmem_limit_bytes=60 * 1024 * 1024
        ),
        cost_estimate=pl.CostEstimate(flops=6 * 512 * 1024 * 2048, bytes_accessed=300000, transcendentals=4096),
    )(example_sketch, candidate_sketch, best_start.reshape(8, 128), chosen)
    return best.reshape(examples), gains


def solution(mesh):
    return jax.shard_map(
        on_device,
        mesh=mesh,
        in_specs=(P("col", "row"), P("row", "col"), P("row"), P()),
        out_specs=(P("row"), P(None, "col")),
        check_vma=False,
    )
```

```python
import functools

import jax
import jax.numpy as jnp
from jax import lax
from jax.experimental import pallas as pl
from jax.experimental.pallas import tpu as pltpu
from jax.sharding import PartitionSpec as P

EPS = 1e-06
LEVELS = 16
GROUP = 32
PIECES = 4
TILE = 256
F32, BF16 = jnp.float32, jnp.bfloat16


def remote(src, dst, send, recv, row, col):
    return pltpu.make_async_remote_copy(
        src_ref=src,
        dst_ref=dst,
        send_sem=send,
        recv_sem=recv,
        device_id={"row": row, "col": col},
        device_id_type=pl.DeviceIdType.MESH,
    )


def slot_rows(slot):
    return pl.ds((slot % LEVELS) * GROUP, GROUP)


def kernel(
    ex_hbm, cand_hbm, best_hbm, chosen_hbm, best_out, gains_out,
    cand, c_hi, c_lo, c_sq, ex, e_hi, e_lo, acc, best_rep, best_in, chosen, ch_part, ch, ch_hi, ch_lo,
    g_own, g_sib, g_all, g_sum,
    loc_sem, ring_s, ring_r, sib_s, sib_r, p1_s, p1_r, p2_s, p2_r, wave,
    cx_s, cx_r, z1_s, z1_r, z2_s, z2_r, gs_s, gs_r, gz_s, gz_r, gf_s, gf_r,
):
    row, col = lax.axis_index("row"), lax.axis_index("col")
    z, c, y, x = row // 2, row % 2, col // 4, col % 4

    def in_x(d):
        return y * 4 + (x + d) % 4

    def in_y(d):
        return ((y + d) % 4) * 4 + x

    def in_z(d):
        return ((z + d + LEVELS) % LEVELS) * 2 + c

    above, below = ((z + 1) % LEVELS) * 2, ((z + LEVELS - 1) % LEVELS) * 2
    sib = z * 2 + 1 - c
    onward = jnp.where(c == 0, above, below + 1)
    sent = []

    def go(*args):
        remote(*args).start()

    def left(view, sem):
        sent.append(remote(view, view, sem, loc_sem.at[0], sib, col))

    def arrived(view, sem):
        remote(view, view, loc_sem.at[0], sem, sib, col).wait_recv()

    barrier = pltpu.get_barrier_semaphore()
    near = [(r, col) for r in (above, above + 1, below, below + 1, sib)]
    near += [(row, t) for d in (1, 2, 3) for t in (in_x(d), in_y(d))]
    for r, t in near:
        pl.semaphore_signal(
            barrier, inc=1, device_id={"row": r, "col": t}, device_id_type=pl.DeviceIdType.MESH
        )

    mine = pl.ds(pl.multiple_of(4 * GROUP + c * 16, 16), 16)

    def ex_view(t, half, rows=16, skip=0):
        slot = (t - z + 4 + LEVELS) % LEVELS
        return ex.at[pl.ds(pl.multiple_of(slot * GROUP + 16 * half + skip, 8), rows)]

    copies = [
        pltpu.make_async_copy(cand_hbm, cand.at[mine], loc_sem.at[0]),
        pltpu.make_async_copy(chosen_hbm, chosen, loc_sem.at[1]),
        pltpu.make_async_copy(ex_hbm, ex_view(col, 0, 32), loc_sem.at[2]),
        pltpu.make_async_copy(best_hbm, best_in, loc_sem.at[3]),
    ]
    for copy in copies:
        copy.start()
    copies[0].wait()
    copies[1].wait()

    lane = lax.broadcasted_iota(jnp.int32, (128, 128), 1)
    sub = lax.broadcasted_iota(jnp.int32, (128, 128), 0)

    block = cand[mine, :]
    wide = lax.broadcasted_iota(jnp.int32, block.shape, 1)
    tile = jnp.zeros((8, 128), F32)
    for r in range(2):
        place = chosen[r] - col * block.shape[1]
        value = jnp.sum(jnp.where(wide == place, block, 0.0), axis=1, keepdims=True)
        line = jnp.sum(
            jnp.where(lane[:16] == sub[:16] + (GROUP * (z % 4) + 16 * c), value, 0.0), axis=0, keepdims=True
        )
        tile = tile + jnp.where(sub[:8] == r, line, 0.0)
    ch_part[0] = tile
    copies[2].wait()
    copies[3].wait()
    pl.semaphore_wait(barrier, len(near))

    def wave_send(i):
        for k, r in enumerate((in_z(1), in_z(-1))):
            pl.semaphore_signal(
                wave.at[i, k], inc=1, device_id={"row": r, "col": col}, device_id_type=pl.DeviceIdType.MESH
            )

    def wave_wait(i):
        pl.semaphore_wait(wave.at[i, 0], 1)
        pl.semaphore_wait(wave.at[i, 1], 1)

    wave_send(0)

    width = cand.shape[1] * 2 // PIECES

    def piece(first_row, half, k):
        start = pl.multiple_of(first_row + 8 * half, 8)
        return cand.at[pl.ds(start, 8), pl.ds((k // 2) * width, width)]

    for k in range(PIECES):
        src = piece(4 * GROUP + c * 16, k % 2, k)
        go(src, piece(3 * GROUP + c * 16, k % 2, k), ring_s.at[0], ring_r.at[0, c, k], above, col)
        go(src, piece(5 * GROUP + c * 16, k % 2, k), ring_s.at[0], ring_r.at[0, c, k], below + 1, col)
    go(cand.at[mine], cand.at[mine], sib_s.at[0], sib_r.at[0], sib, col)
    left(cand.at[pl.ds(0, 32)], ring_s.at[0])
    left(cand.at[pl.ds(0, 16)], sib_s.at[0])
    two = pl.ds(0, 2)
    for j in range(3):
        go(ch_part.at[0, two], ch_part.at[2 + j, two], cx_s.at[0], cx_r.at[0, j], row, in_x(j + 1))
    left(ch.at[pl.ds(0, 3), two], cx_s.at[0])

    lines = ((in_x, in_y), (in_y, in_x))

    def spread(half, phase, i, view):
        s, r = (p1_s, p1_r) if phase == 0 else (p2_s, p2_r)
        for k, d in enumerate((1, 3)):
            go(view, view, s.at[half, i], r.at[half, i, k], row, lines[half][phase](d))
        left(ex.at[pl.ds(0, 48)], s.at[half, i])

    def relay(half, phase, i, k, owner):
        s, r = (p1_s, p1_r) if phase == 0 else (p2_s, p2_r)
        arrived(ex_view(owner, half), r.at[half, i, k])
        view = ex_view(owner, half, 8, 8 * k)
        go(view, view, s.at[half, i], r.at[half, i, 2 + k], row, lines[half][phase]((1, 3)[k]))

    def opposite(half, phase, i):
        r = p1_r if phase == 0 else p2_r
        arrived(ex.at[pl.ds(0, 8)], r.at[half, i, 2])
        arrived(ex.at[pl.ds(0, 8)], r.at[half, i, 3])

    def first(half, d):
        return lines[half][0](d)

    def second(half, d1, d2):
        xx, yy = (d1, d2) if half == 0 else (d2, d1)
        return ((y + yy) % 4) * 4 + (x + xx) % 4

    for half in range(2):
        spread(half, 0, 0, ex_view(col, half))
    for half in range(2):
        spread(half, 1, 0, ex_view(col, half))

    plan = {}

    def at(h, i, *fns):
        plan.setdefault((h, i), []).extend(fns)

    def call(fn, *args):
        return functools.partial(fn, *args)

    def phase_one(half, k):
        d = (3, 1)[k]
        relay(half, 0, 0, k, first(half, d))
        spread(half, 1, d, ex_view(first(half, d), half))

    def phase_one_far(half):
        opposite(half, 0, 0)
        spread(half, 1, 2, ex_view(first(half, 2), half))

    def phase_two(half, d, k):
        relay(half, 1, d, k, second(half, d, (3, 1)[k]))

    def from_sib(h):
        arrived(cand.at[pl.ds(0, 16 if h in (0, 8) else GROUP)], sib_r.at[h])

    def prepare(slot):
        v = cand[slot_rows(slot), :]
        hi = v.astype(BF16)
        c_hi[slot_rows(slot), :] = hi
        c_lo[slot_rows(slot), :] = (v - hi.astype(F32)).astype(BF16)
        sq = v * v
        c_sq[...] += sq[0:8] + sq[8:16] + sq[16:24] + sq[24:32]

    def chosen_y():
        for j in range(3):
            arrived(ch_part.at[2 + j, two], cx_r.at[0, j])
        ch_part[1, two] = ch_part[0, two] + ch_part[2, two] + ch_part[3, two] + ch_part[4, two]
        for j in range(3):
            go(ch_part.at[1, two], ch_part.at[5 + j, two], cx_s.at[1], cx_r.at[1, j], row, in_y(j + 1))
        left(ch.at[pl.ds(0, 3), two], cx_s.at[1])

    def chosen_sib():
        for j in range(3):
            arrived(ch_part.at[5 + j, two], cx_r.at[1, j])
        ch_part[8, two] = ch_part[1, two] + ch_part[5, two] + ch_part[6, two] + ch_part[7, two]
        go(ch_part.at[8, two], ch_part.at[9, two], cx_s.at[2], cx_r.at[2, 0], sib, col)
        left(ch.at[0, two], cx_s.at[2])

    def chosen_near():
        arrived(ch_part.at[9, two], cx_r.at[2, 0])
        ch[4, two] = ch_part[8, two] + ch_part[9, two]
        for d in range(1, 5):
            go(ch.at[4, two], ch.at[4 - d, two], z1_s.at[0], z1_r.at[0], in_z(d), col)
            go(ch.at[4, two], ch.at[4 + d, two], z1_s.at[1], z1_r.at[1], in_z(-d), col)
        left(ch.at[pl.ds(0, 4), two], z1_s.at[0])
        left(ch.at[pl.ds(0, 4), two], z1_s.at[1])

    def chosen_far():
        arrived(ch.at[pl.ds(0, 4), two], z1_r.at[0])
        arrived(ch.at[pl.ds(0, 4), two], z1_r.at[1])
        go(ch.at[pl.ds(0, 4), two], ch.at[pl.ds(12, 4), two], z2_s.at[0], z2_r.at[0], in_z(4), col)
        go(ch.at[pl.ds(5, 3), two], ch.at[pl.ds(9, 3), two], z2_s.at[1], z2_r.at[1], in_z(-4), col)
        left(ch.at[pl.ds(0, 4), two], z2_s.at[0])
        left(ch.at[pl.ds(0, 3), two], z2_s.at[1])

    held = {"e_sq": jnp.zeros((8, ex.shape[1]), F32), "ch_sq": [jnp.zeros((1, 128), F32)] * 2}

    def square(part):
        total = held["e_sq"]
        for i in range(32 * part, 32 * part + 32):
            v = ex[pl.ds(8 * i, 8), :]
            total = total + v * v
        held["e_sq"] = total
        if part == 1:
            scale = jnp.sqrt(jnp.float32(LEVELS * GROUP))
            held["factor"] = scale / jnp.sqrt(jnp.sum(total, axis=0, keepdims=True) + EPS)

    def turn(i, q):
        v = ex[pl.ds(128 * q, 128), pl.ds(128 * i, 128)] * held["factor"][:, 128 * i : 128 * (i + 1)]
        v = v.T
        hi = v.astype(BF16)
        e_hi[pl.ds(128 * i, 128), pl.ds(128 * q, 128)] = hi
        e_lo[pl.ds(128 * i, 128), pl.ds(128 * q, 128)] = (v - hi.astype(F32)).astype(BF16)

    def chosen_wide(q):
        four = ch[4 * q, two] + ch[4 * q + 1, two] + ch[4 * q + 2, two] + ch[4 * q + 3, two]
        for r in range(2):
            v = jnp.broadcast_to(four[r : r + 1, :], (128, 128)).T
            held["ch_sq"] = [
                s + jnp.sum(v * v, axis=0, keepdims=True) if k == r else s for k, s in enumerate(held["ch_sq"])
            ]
            hi = v.astype(BF16)
            lo = (v - hi.astype(F32)).astype(BF16)
            for b in range(4):
                to = pl.ds(pl.multiple_of(((b - z + LEVELS) % 4 + 4 * q) * GROUP, GROUP), GROUP)
                ch_hi[to, pl.ds(128 * r, 128)] = hi[32 * b : 32 * b + 32]
                ch_lo[to, pl.ds(128 * r, 128)] = lo[32 * b : 32 * b + 32]

    def chosen_come():
        arrived(ch.at[pl.ds(0, 4), two], z2_r.at[0])
        arrived(ch.at[pl.ds(0, 3), two], z2_r.at[1])

    dot = functools.partial(jnp.dot, preferred_element_type=F32)

    def pick(i):
        rows = pl.ds(i * 256, 256)
        hi, lo = e_hi[rows, :], e_lo[rows, :]
        d = dot(hi, ch_hi[...]) + dot(lo, ch_hi[...]) + dot(hi, ch_lo[...])
        b = best_rep[0, rows, :]
        for r in range(2):
            b = jnp.maximum(b, d[:, 128 * r : 128 * r + 128] / jnp.sqrt(held["ch_sq"][r] + EPS))
            best_rep[r, rows, :] = b
        for k in range(2):
            best_out[pl.ds(2 * i + k, 1), :] = jnp.sum(
                jnp.where(lane == sub, b[128 * k : 128 * k + 128], 0.0), axis=0, keepdims=True
            )

    def first_half(n, m):
        cols, rows = pl.ds(n * TILE, TILE), pl.ds(m * 512, 512)
        hi, lo = c_hi[pl.ds(0, 256), cols], c_lo[pl.ds(0, 256), cols]
        a_hi, a_lo = e_hi[rows, pl.ds(0, 256)], e_lo[rows, pl.ds(0, 256)]
        acc[rows, cols] = dot(a_hi, hi) + dot(a_lo, hi) + dot(a_hi, lo)

    at(1, 3, call(wave_wait, 2), chosen_y)
    at(2, 7, chosen_sib)
    at(3, 3, chosen_near)
    at(5, 4, chosen_far)
    at(7, 2, chosen_come, call(chosen_wide, 0))
    at(7, 3, call(chosen_wide, 1))
    at(7, 4, call(chosen_wide, 2))
    at(7, 5, call(chosen_wide, 3))
    for n, (half, k) in enumerate(((0, 0), (0, 1), (1, 0), (1, 1))):
        at(1, (1, 2, 4, 5)[n], call(phase_one, half, k))
        at(2, n, call(phase_two, half, 0, k))
        at(3, 2 * (n % 2) + 1, call(phase_two, half, 1, k))
        at(3, 2 * (n % 2) + 4, call(phase_two, half, 3, k))
        at(4, n, call(phase_two, half, 2, k))
    at(2, 5, call(phase_one_far, 0))
    at(2, 6, call(phase_one_far, 1))
    for half in range(2):
        for d in range(4):
            at(5, 0, call(opposite, half, 1, d))
    at(5, 1, call(square, 0))
    at(5, 2, call(square, 1))
    work = [call(turn, i, q) for q in range(2) for i in range(8)]
    for i, fn in enumerate(work):
        at(5, 3 + i // 4, fn)
    work = [call(turn, i, q) for q in range(2, 4) for i in range(8)]
    for i, fn in enumerate(work):
        at(6, 6 + i // 8, fn)
    for h in range(1, 7):
        at(h + 1, 3, call(from_sib, h))
        at(h + 1, 4, call(prepare, (4 - h) % LEVELS))
        at(h + 1, 5, call(prepare, 4 + h))
    halves = [(n, m) for n in range(8) for m in range(2)]
    for i, (n, m) in enumerate(halves[:6]):
        at(6, i, call(first_half, n, m))
    for i, (n, m) in enumerate(halves[6:14]):
        at(7, i, call(first_half, n, m))
    for i, (n, m) in enumerate(halves[14:]):
        at(8, i, call(first_half, n, m))
    for i in range(4):
        at(7, 6 + i // 2, call(pick, i))

    c_sq[...] = jnp.zeros_like(c_sq)
    for i in range(8):
        best_rep[0, pl.ds(128 * i, 128), :] = jnp.broadcast_to(best_in[pl.ds(i, 1), :], (128, 128)).T
    wave_wait(0)
    wave_send(1)
    from_sib(0)
    prepare(4)
    wave_wait(1)
    wave_send(2)

    for h in range(1, 9):
        base = jnp.where(c == 0, ((4 - h) % LEVELS) * GROUP, ((4 + h) % LEVELS) * GROUP)
        after = jnp.where(c == 0, ((3 - h) % LEVELS) * GROUP, ((5 + h) % LEVELS) * GROUP)
        event = 0
        for k in range(PIECES):
            for o in range(2):
                far = k % 2 == 0
                if h == 8 and not far:
                    continue
                half = (k % 2 + c) % 2
                view = piece(base + o * 16, half, k)
                kk = (k // 2) * 2 + half if h == 1 else k
                arrived(view, ring_r.at[h - 1, o, kk])
                if h < 7 or (far and h < 8):
                    go(view, piece(after + o * 16, half, k), ring_s.at[h], ring_r.at[h, o, k], onward, col)
                go(view, view, sib_s.at[h], sib_r.at[h], sib, col)
                for fn in plan.pop((h, event), ()):
                    fn()
                event += 1
        if h < 8:
            left(cand.at[pl.ds(0, 32 if h < 7 else 16)], ring_s.at[h])
        left(cand.at[pl.ds(0, 32 if h < 8 else 16)], sib_s.at[h])
    assert not plan
    from_sib(7)
    prepare(13)
    prepare(11)
    from_sib(8)
    prepare(12)

    def second_half(n, _):
        cols = pl.ds(pl.multiple_of(n * TILE, TILE), TILE)
        hi, lo = c_hi[pl.ds(256, 256), cols], c_lo[pl.ds(256, 256), cols]
        a_hi, a_lo = e_hi[:, pl.ds(256, 256)], e_lo[:, pl.ds(256, 256)]
        d = acc[:, cols] + (dot(a_hi, hi) + dot(a_lo, hi) + dot(a_hi, lo))
        norm = jnp.sqrt(jnp.sum(c_sq[:, cols], axis=0, keepdims=True) + EPS)
        sim = d * (1.0 / norm)
        for r in range(2):
            b = best_rep[r]
            for t in range(2):
                part = jnp.maximum(sim[:, 128 * t : 128 * t + 128] - b, 0.0)
                g_own[r, pl.ds(2 * n + t, 1), :] = jnp.sum(part, axis=0, keepdims=True)
        return 0

    def rows_of(p):
        return pl.ds(4 * p, 4)

    def to_sib(p):
        go(g_own.at[1 - c, rows_of(p)], g_sib.at[rows_of(p)], gs_s.at[p], gs_r.at[p], sib, col)
        left(g_sib.at[rows_of(p)], gs_s.at[p])

    def to_levels(p):
        part = rows_of(p)
        arrived(g_sib.at[part], gs_r.at[p])
        g_all[0, part] = g_own[c, part] + g_sib[part]
        for d in (8, 7, 9, 6, 10, 5, 11, 4, 12, 3, 13, 2, 14, 1, 15):
            go(g_all.at[0, part], g_all.at[d, part], gz_s.at[p], gz_r.at[p], in_z(d), col)
        left(g_all.at[pl.ds(1, 15), part], gz_s.at[p])

    for p in range(4):
        lax.fori_loop(2 * p, 2 * p + 2, second_half, 0)
        to_sib(p)
        if p > 0:
            to_levels(p - 1)
    to_levels(3)
    for copy in sent:
        copy.wait_send()
    for p in range(4):
        arrived(g_all.at[pl.ds(1, 15), rows_of(p)], gz_r.at[p])
    total = g_all[0]
    for d in range(1, LEVELS):
        total = total + g_all[d]
    g_sum[c] = total
    go(g_sum.at[c], g_sum.at[c], gf_s, gf_r, sib, col)
    arrived(g_sum.at[1 - c], gf_r)
    for r in range(2):
        for t in range(16):
            gains_out[pl.ds(r, 1), pl.ds(128 * t, 128)] = g_sum[r, pl.ds(t, 1), :]
    remote(g_sum.at[c], g_sum.at[c], gf_s, gf_r, sib, col).wait_send()


def on_device(example_sketch, candidate_sketch, best_start, chosen):
    dma = pltpu.SemaphoreType.DMA
    vmem = pltpu.VMEM
    examples, candidates = example_sketch.shape[1], candidate_sketch.shape[1]
    widths = LEVELS * GROUP
    best, gains = pl.pallas_call(
        kernel,
        out_shape=(
            jax.ShapeDtypeStruct((8, 128), F32),
            jax.ShapeDtypeStruct((2, candidates), F32),
        ),
        in_specs=[
            pl.BlockSpec(memory_space=pltpu.HBM),
            pl.BlockSpec(memory_space=pltpu.HBM),
            pl.BlockSpec(memory_space=pltpu.HBM),
            pl.BlockSpec(memory_space=pltpu.HBM),
        ],
        out_specs=(pl.BlockSpec(memory_space=pltpu.VMEM), pl.BlockSpec(memory_space=pltpu.VMEM)),
        scratch_shapes=[
            vmem((widths, candidates), F32),
            vmem((widths, candidates), BF16),
            vmem((widths, candidates), BF16),
            vmem((8, candidates), F32),
            vmem((widths, examples), F32),
            vmem((examples, widths), BF16),
            vmem((examples, widths), BF16),
            vmem((examples, candidates), F32),
            vmem((2, examples, 128), F32),
            vmem((8, 128), F32),
            pltpu.SMEM((2,), jnp.int32),
            vmem((10, 8, 128), F32),
            vmem((LEVELS, 8, 128), F32),
            vmem((widths, 256), BF16),
            vmem((widths, 256), BF16),
            vmem((2, 16, 128), F32),
            vmem((16, 128), F32),
            vmem((LEVELS, 16, 128), F32),
            vmem((2, 16, 128), F32),
            dma((4,)),
            dma((8,)),
            dma((8, 2, PIECES)),
            dma((9,)),
            dma((9,)),
            dma((2, 1)),
            dma((2, 1, 4)),
            dma((2, 4)),
            dma((2, 4, 4)),
            pltpu.SemaphoreType.REGULAR((3, 2)),
            dma((3,)),
            dma((3, 3)),
            dma((2,)),
            dma((2,)),
            dma((2,)),
            dma((2,)),
            dma((4,)),
            dma((4,)),
            dma((4,)),
            dma((4,)),
            dma,
            dma,
        ],
        compiler_params=pltpu.CompilerParams(
            collective_id=0, has_side_effects=True, vmem_limit_bytes=60 * 1024 * 1024
        ),
        cost_estimate=pl.CostEstimate(flops=6 * 512 * 1024 * 2048, bytes_accessed=300000, transcendentals=4096),
    )(example_sketch, candidate_sketch, best_start.reshape(8, 128), chosen)
    return jnp.maximum(best.reshape(examples), best_start), gains * (1.0 / 32768.0)


def solution(mesh):
    return jax.shard_map(
        on_device,
        mesh=mesh,
        in_specs=(P("col", "row"), P("row", "col"), P("row"), P()),
        out_specs=(P("row"), P(None, "col")),
        check_vma=False,
    )
```

```python
import functools

import jax
import jax.numpy as jnp
from jax import lax
from jax.experimental import pallas as pl
from jax.experimental.pallas import tpu as pltpu
from jax.sharding import PartitionSpec as P

EPS = 1e-06
LEVELS = 16
GROUP = 32
PIECES = 4
TILE = 256
F32, BF16 = jnp.float32, jnp.bfloat16


def remote(src, dst, send, recv, row, col):
    return pltpu.make_async_remote_copy(
        src_ref=src,
        dst_ref=dst,
        send_sem=send,
        recv_sem=recv,
        device_id={"row": row, "col": col},
        device_id_type=pl.DeviceIdType.MESH,
    )


def slot_rows(slot):
    return pl.ds((slot % LEVELS) * GROUP, GROUP)


def kernel(
    ex_hbm, cand_hbm, best_hbm, chosen_hbm, best_out, gains_out,
    cand, c_hi, c_lo, c_sq, ex, e_hi, e_lo, acc, best_rep, best_in, chosen, ch_part, ch, ch_hi, ch_lo,
    g_own, g_sib, g_all, g_sum,
    loc_sem, ring_s, ring_r, sib_s, sib_r, p1_s, p1_r, p2_s, p2_r, wave,
    cx_s, cx_r, z1_s, z1_r, z2_s, z2_r, gs_s, gs_r, gz_s, gz_r, gf_s, gf_r,
):
    row, col = lax.axis_index("row"), lax.axis_index("col")
    z, c, y, x = row // 2, row % 2, col // 4, col % 4

    def in_x(d):
        return y * 4 + (x + d) % 4

    def in_y(d):
        return ((y + d) % 4) * 4 + x

    def in_z(d):
        return ((z + d + LEVELS) % LEVELS) * 2 + c

    above, below = ((z + 1) % LEVELS) * 2, ((z + LEVELS - 1) % LEVELS) * 2
    sib = z * 2 + 1 - c
    onward = jnp.where(c == 0, above, below + 1)
    sent = []

    def go(*args):
        remote(*args).start()

    def left(view, sem):
        sent.append(remote(view, view, sem, loc_sem.at[0], sib, col))

    def arrived(view, sem):
        remote(view, view, loc_sem.at[0], sem, sib, col).wait_recv()

    barrier = pltpu.get_barrier_semaphore()
    near = [(r, col) for r in (above, above + 1, below, below + 1, sib)]
    near += [(row, t) for d in (1, 2, 3) for t in (in_x(d), in_y(d))]
    for r, t in near:
        pl.semaphore_signal(
            barrier, inc=1, device_id={"row": r, "col": t}, device_id_type=pl.DeviceIdType.MESH
        )

    mine = pl.ds(pl.multiple_of(4 * GROUP + c * 16, 16), 16)

    def ex_view(t, half, rows=16, skip=0):
        slot = (t - z + 4 + LEVELS) % LEVELS
        return ex.at[pl.ds(pl.multiple_of(slot * GROUP + 16 * half + skip, 8), rows)]

    copies = [
        pltpu.make_async_copy(cand_hbm, cand.at[mine], loc_sem.at[0]),
        pltpu.make_async_copy(chosen_hbm, chosen, loc_sem.at[1]),
        pltpu.make_async_copy(ex_hbm, ex_view(col, 0, 32), loc_sem.at[2]),
        pltpu.make_async_copy(best_hbm, best_in, loc_sem.at[3]),
    ]
    for copy in copies:
        copy.start()
    copies[0].wait()
    copies[1].wait()

    lane = lax.broadcasted_iota(jnp.int32, (128, 128), 1)
    sub = lax.broadcasted_iota(jnp.int32, (128, 128), 0)

    block = cand[mine, :]
    wide = lax.broadcasted_iota(jnp.int32, block.shape, 1)
    tile = jnp.zeros((8, 128), F32)
    for r in range(2):
        place = chosen[r] - col * block.shape[1]
        value = jnp.sum(jnp.where(wide == place, block, 0.0), axis=1, keepdims=True)
        line = jnp.sum(
            jnp.where(lane[:16] == sub[:16] + (GROUP * (z % 4) + 16 * c), value, 0.0), axis=0, keepdims=True
        )
        tile = tile + jnp.where(sub[:8] == r, line, 0.0)
    ch_part[0] = tile
    copies[2].wait()
    copies[3].wait()
    pl.semaphore_wait(barrier, len(near))

    def wave_send(i):
        for k, r in enumerate((in_z(1), in_z(-1))):
            pl.semaphore_signal(
                wave.at[i, k], inc=1, device_id={"row": r, "col": col}, device_id_type=pl.DeviceIdType.MESH
            )

    def wave_wait(i):
        pl.semaphore_wait(wave.at[i, 0], 1)
        pl.semaphore_wait(wave.at[i, 1], 1)

    wave_send(0)

    width = cand.shape[1] * 2 // PIECES

    def piece(first_row, half, k):
        start = pl.multiple_of(first_row + 8 * half, 8)
        return cand.at[pl.ds(start, 8), pl.ds((k // 2) * width, width)]

    for k in range(PIECES):
        src = piece(4 * GROUP + c * 16, k % 2, k)
        go(src, piece(3 * GROUP + c * 16, k % 2, k), ring_s.at[0], ring_r.at[0, c, k], above, col)
        go(src, piece(5 * GROUP + c * 16, k % 2, k), ring_s.at[0], ring_r.at[0, c, k], below + 1, col)
    go(cand.at[mine], cand.at[mine], sib_s.at[0], sib_r.at[0], sib, col)
    left(cand.at[pl.ds(0, 32)], ring_s.at[0])
    left(cand.at[pl.ds(0, 16)], sib_s.at[0])
    two = pl.ds(0, 2)
    for j in range(3):
        go(ch_part.at[0, two], ch_part.at[2 + j, two], cx_s.at[0], cx_r.at[0, j], row, in_x(j + 1))
    left(ch.at[pl.ds(0, 3), two], cx_s.at[0])

    lines = ((in_x, in_y), (in_y, in_x))

    def spread(half, phase, i, view):
        s, r = (p1_s, p1_r) if phase == 0 else (p2_s, p2_r)
        for k, d in enumerate((1, 3)):
            go(view, view, s.at[half, i], r.at[half, i, k], row, lines[half][phase](d))
        left(ex.at[pl.ds(0, 48)], s.at[half, i])

    def relay(half, phase, i, k, owner):
        s, r = (p1_s, p1_r) if phase == 0 else (p2_s, p2_r)
        arrived(ex_view(owner, half), r.at[half, i, k])
        view = ex_view(owner, half, 8, 8 * k)
        go(view, view, s.at[half, i], r.at[half, i, 2 + k], row, lines[half][phase]((1, 3)[k]))

    def opposite(half, phase, i):
        r = p1_r if phase == 0 else p2_r
        arrived(ex.at[pl.ds(0, 8)], r.at[half, i, 2])
        arrived(ex.at[pl.ds(0, 8)], r.at[half, i, 3])

    def first(half, d):
        return lines[half][0](d)

    def second(half, d1, d2):
        xx, yy = (d1, d2) if half == 0 else (d2, d1)
        return ((y + yy) % 4) * 4 + (x + xx) % 4

    for half in range(2):
        spread(half, 0, 0, ex_view(col, half))
    for half in range(2):
        spread(half, 1, 0, ex_view(col, half))

    plan = {}

    def at(h, i, *fns):
        i = 7 if 4 < h < 8 else 3 if h == 8 else i
        plan.setdefault((h, i), []).extend(fns)

    def call(fn, *args):
        return functools.partial(fn, *args)

    def phase_one(half, k):
        d = (3, 1)[k]
        relay(half, 0, 0, k, first(half, d))
        spread(half, 1, d, ex_view(first(half, d), half))

    def phase_one_far(half):
        opposite(half, 0, 0)
        spread(half, 1, 2, ex_view(first(half, 2), half))

    def phase_two(half, d, k):
        relay(half, 1, d, k, second(half, d, (3, 1)[k]))

    def from_sib(h):
        arrived(cand.at[pl.ds(0, 16 if h in (0, 8) else GROUP)], sib_r.at[h])

    def prepare(slot):
        v = cand[slot_rows(slot), :]
        hi = v.astype(BF16)
        c_hi[slot_rows(slot), :] = hi
        c_lo[slot_rows(slot), :] = (v - hi.astype(F32)).astype(BF16)
        sq = v * v
        c_sq[...] += sq[0:8] + sq[8:16] + sq[16:24] + sq[24:32]

    def chosen_y():
        for j in range(3):
            arrived(ch_part.at[2 + j, two], cx_r.at[0, j])
        ch_part[1, two] = ch_part[0, two] + ch_part[2, two] + ch_part[3, two] + ch_part[4, two]
        for j in range(3):
            go(ch_part.at[1, two], ch_part.at[5 + j, two], cx_s.at[1], cx_r.at[1, j], row, in_y(j + 1))
        left(ch.at[pl.ds(0, 3), two], cx_s.at[1])

    def chosen_sib():
        for j in range(3):
            arrived(ch_part.at[5 + j, two], cx_r.at[1, j])
        ch_part[8, two] = ch_part[1, two] + ch_part[5, two] + ch_part[6, two] + ch_part[7, two]
        go(ch_part.at[8, two], ch_part.at[9, two], cx_s.at[2], cx_r.at[2, 0], sib, col)
        left(ch.at[0, two], cx_s.at[2])

    def chosen_near():
        arrived(ch_part.at[9, two], cx_r.at[2, 0])
        ch[4, two] = ch_part[8, two] + ch_part[9, two]
        for d in range(1, 5):
            go(ch.at[4, two], ch.at[4 - d, two], z1_s.at[0], z1_r.at[0], in_z(d), col)
            go(ch.at[4, two], ch.at[4 + d, two], z1_s.at[1], z1_r.at[1], in_z(-d), col)
        left(ch.at[pl.ds(0, 4), two], z1_s.at[0])
        left(ch.at[pl.ds(0, 4), two], z1_s.at[1])

    def chosen_far():
        arrived(ch.at[pl.ds(0, 4), two], z1_r.at[0])
        arrived(ch.at[pl.ds(0, 4), two], z1_r.at[1])
        go(ch.at[pl.ds(0, 4), two], ch.at[pl.ds(12, 4), two], z2_s.at[0], z2_r.at[0], in_z(4), col)
        go(ch.at[pl.ds(5, 3), two], ch.at[pl.ds(9, 3), two], z2_s.at[1], z2_r.at[1], in_z(-4), col)
        left(ch.at[pl.ds(0, 4), two], z2_s.at[0])
        left(ch.at[pl.ds(0, 3), two], z2_s.at[1])

    held = {"e_sq": jnp.zeros((8, ex.shape[1]), F32), "ch_sq": [jnp.zeros((1, 128), F32)] * 2}

    def square(part):
        total = held["e_sq"]
        for i in range(32 * part, 32 * part + 32):
            v = ex[pl.ds(8 * i, 8), :]
            total = total + v * v
        held["e_sq"] = total
        if part == 1:
            scale = jnp.sqrt(jnp.float32(LEVELS * GROUP))
            held["factor"] = scale / jnp.sqrt(jnp.sum(total, axis=0, keepdims=True) + EPS)

    def turn(i, q):
        v = ex[pl.ds(128 * q, 128), pl.ds(128 * i, 128)] * held["factor"][:, 128 * i : 128 * (i + 1)]
        v = v.T
        hi = v.astype(BF16)
        e_hi[pl.ds(128 * i, 128), pl.ds(128 * q, 128)] = hi
        e_lo[pl.ds(128 * i, 128), pl.ds(128 * q, 128)] = (v - hi.astype(F32)).astype(BF16)

    def chosen_wide(q):
        four = ch[4 * q, two] + ch[4 * q + 1, two] + ch[4 * q + 2, two] + ch[4 * q + 3, two]
        for r in range(2):
            v = jnp.broadcast_to(four[r : r + 1, :], (128, 128)).T
            held["ch_sq"] = [
                s + jnp.sum(v * v, axis=0, keepdims=True) if k == r else s for k, s in enumerate(held["ch_sq"])
            ]
            hi = v.astype(BF16)
            lo = (v - hi.astype(F32)).astype(BF16)
            for b in range(4):
                to = pl.ds(pl.multiple_of(((b - z + LEVELS) % 4 + 4 * q) * GROUP, GROUP), GROUP)
                ch_hi[to, pl.ds(128 * r, 128)] = hi[32 * b : 32 * b + 32]
                ch_lo[to, pl.ds(128 * r, 128)] = lo[32 * b : 32 * b + 32]

    def chosen_come():
        arrived(ch.at[pl.ds(0, 4), two], z2_r.at[0])
        arrived(ch.at[pl.ds(0, 3), two], z2_r.at[1])

    dot = functools.partial(jnp.dot, preferred_element_type=F32)

    def pick(i):
        rows = pl.ds(i * 256, 256)
        hi, lo = e_hi[rows, :], e_lo[rows, :]
        d = dot(hi, ch_hi[...]) + dot(lo, ch_hi[...]) + dot(hi, ch_lo[...])
        b = best_rep[0, rows, :]
        for r in range(2):
            b = jnp.maximum(b, d[:, 128 * r : 128 * r + 128] / jnp.sqrt(held["ch_sq"][r] + EPS))
            best_rep[r, rows, :] = b
        for k in range(2):
            best_out[pl.ds(2 * i + k, 1), :] = jnp.sum(
                jnp.where(lane == sub, b[128 * k : 128 * k + 128], 0.0), axis=0, keepdims=True
            )

    def first_half(n, m):
        cols, rows = pl.ds(n * TILE, TILE), pl.ds(m * 512, 512)
        hi, lo = c_hi[pl.ds(0, 256), cols], c_lo[pl.ds(0, 256), cols]
        a_hi, a_lo = e_hi[rows, pl.ds(0, 256)], e_lo[rows, pl.ds(0, 256)]
        acc[rows, cols] = dot(a_hi, hi) + dot(a_lo, hi) + dot(a_hi, lo)

    at(1, 3, call(wave_wait, 2), chosen_y)
    at(2, 7, chosen_sib)
    at(3, 3, chosen_near)
    at(5, 4, chosen_far)
    at(7, 2, chosen_come, call(chosen_wide, 0))
    at(7, 3, call(chosen_wide, 1))
    at(7, 4, call(chosen_wide, 2))
    at(7, 5, call(chosen_wide, 3))
    for n, (half, k) in enumerate(((0, 0), (0, 1), (1, 0), (1, 1))):
        at(1, (1, 2, 4, 5)[n], call(phase_one, half, k))
        at(2, n, call(phase_two, half, 0, k))
        at(3, 2 * (n % 2) + 1, call(phase_two, half, 1, k))
        at(3, 2 * (n % 2) + 4, call(phase_two, half, 3, k))
        at(4, n, call(phase_two, half, 2, k))
    at(2, 5, call(phase_one_far, 0))
    at(2, 6, call(phase_one_far, 1))
    for half in range(2):
        for d in range(4):
            at(5, 0, call(opposite, half, 1, d))
    at(5, 1, call(square, 0))
    at(5, 2, call(square, 1))
    work = [call(turn, i, q) for q in range(2) for i in range(8)]
    for i, fn in enumerate(work):
        at(5, 3 + i // 4, fn)
    work = [call(turn, i, q) for q in range(2, 4) for i in range(8)]
    for i, fn in enumerate(work):
        at(6, 6 + i // 8, fn)
    for h in range(1, 7):
        at(h + 1, 3, call(from_sib, h))
        at(h + 1, 4, call(prepare, (4 - h) % LEVELS))
        at(h + 1, 5, call(prepare, 4 + h))
    halves = [(n, m) for n in range(8) for m in range(2)]
    for i, (n, m) in enumerate(halves[:3]):
        at(6, i, call(first_half, n, m))
    for i, (n, m) in enumerate(halves[3:8]):
        at(7, i, call(first_half, n, m))
    for i, (n, m) in enumerate(halves[8:]):
        at(8, 3, call(first_half, n, m))
    for i in range(4):
        at(7, 6 + i // 2, call(pick, i))

    c_sq[...] = jnp.zeros_like(c_sq)
    for i in range(8):
        best_rep[0, pl.ds(128 * i, 128), :] = jnp.broadcast_to(best_in[pl.ds(i, 1), :], (128, 128)).T
    wave_wait(0)
    wave_send(1)
    from_sib(0)
    prepare(4)
    wave_wait(1)
    wave_send(2)

    for h in range(1, 9):
        base = jnp.where(c == 0, ((4 - h) % LEVELS) * GROUP, ((4 + h) % LEVELS) * GROUP)
        after = jnp.where(c == 0, ((3 - h) % LEVELS) * GROUP, ((5 + h) % LEVELS) * GROUP)
        event = 0
        for k in range(PIECES):
            for o in range(2):
                far = k % 2 == 0
                if h == 8 and not far:
                    continue
                half = (k % 2 + c) % 2
                view = piece(base + o * 16, half, k)
                kk = (k // 2) * 2 + half if h == 1 else k
                arrived(view, ring_r.at[h - 1, o, kk])
                if h < 7 or (far and h < 8):
                    go(view, piece(after + o * 16, half, k), ring_s.at[h], ring_r.at[h, o, k], onward, col)
                go(view, view, sib_s.at[h], sib_r.at[h], sib, col)
                for fn in plan.pop((h, event), ()):
                    fn()
                event += 1
        if h < 8:
            left(cand.at[pl.ds(0, 32 if h < 7 else 16)], ring_s.at[h])
        left(cand.at[pl.ds(0, 32 if h < 8 else 16)], sib_s.at[h])
    assert not plan
    from_sib(7)
    prepare(13)
    prepare(11)
    from_sib(8)
    prepare(12)

    def second_half(n, _):
        cols = pl.ds(pl.multiple_of(n * TILE, TILE), TILE)
        hi, lo = c_hi[pl.ds(256, 256), cols], c_lo[pl.ds(256, 256), cols]
        a_hi, a_lo = e_hi[:, pl.ds(256, 256)], e_lo[:, pl.ds(256, 256)]
        d = acc[:, cols] + (dot(a_hi, hi) + dot(a_lo, hi) + dot(a_hi, lo))
        norm = jnp.sqrt(jnp.sum(c_sq[:, cols], axis=0, keepdims=True) + EPS)
        sim = d * (1.0 / norm)
        for r in range(2):
            b = best_rep[r]
            for t in range(2):
                part = jnp.maximum(sim[:, 128 * t : 128 * t + 128] - b, 0.0)
                g_own[r, pl.ds(2 * n + t, 1), :] = jnp.sum(part, axis=0, keepdims=True)
        return 0

    def rows_of(p):
        return pl.ds(4 * p, 4)

    def to_sib(p):
        go(g_own.at[1 - c, rows_of(p)], g_sib.at[rows_of(p)], gs_s.at[p], gs_r.at[p], sib, col)
        left(g_sib.at[rows_of(p)], gs_s.at[p])

    def to_levels(p):
        part = rows_of(p)
        arrived(g_sib.at[part], gs_r.at[p])
        g_all[0, part] = g_own[c, part] + g_sib[part]
        for d in (8, 7, 9, 6, 10, 5, 11, 4, 12, 3, 13, 2, 14, 1, 15):
            go(g_all.at[0, part], g_all.at[d, part], gz_s.at[p], gz_r.at[p], in_z(d), col)
        left(g_all.at[pl.ds(1, 15), part], gz_s.at[p])

    for p in range(4):
        lax.fori_loop(2 * p, 2 * p + 2, second_half, 0)
        to_sib(p)
        if p > 0:
            to_levels(p - 1)
    to_levels(3)
    for copy in sent:
        copy.wait_send()
    for p in range(4):
        arrived(g_all.at[pl.ds(1, 15), rows_of(p)], gz_r.at[p])
    total = g_all[0]
    for d in range(1, LEVELS):
        total = total + g_all[d]
    g_sum[c] = total
    go(g_sum.at[c], g_sum.at[c], gf_s, gf_r, sib, col)
    arrived(g_sum.at[1 - c], gf_r)
    for r in range(2):
        for t in range(16):
            gains_out[pl.ds(r, 1), pl.ds(128 * t, 128)] = g_sum[r, pl.ds(t, 1), :]
    remote(g_sum.at[c], g_sum.at[c], gf_s, gf_r, sib, col).wait_send()


def on_device(example_sketch, candidate_sketch, best_start, chosen):
    dma = pltpu.SemaphoreType.DMA
    vmem = pltpu.VMEM
    examples, candidates = example_sketch.shape[1], candidate_sketch.shape[1]
    widths = LEVELS * GROUP
    best, gains = pl.pallas_call(
        kernel,
        out_shape=(
            jax.ShapeDtypeStruct((8, 128), F32),
            jax.ShapeDtypeStruct((2, candidates), F32),
        ),
        in_specs=[
            pl.BlockSpec(memory_space=pltpu.HBM),
            pl.BlockSpec(memory_space=pltpu.HBM),
            pl.BlockSpec(memory_space=pltpu.HBM),
            pl.BlockSpec(memory_space=pltpu.HBM),
        ],
        out_specs=(pl.BlockSpec(memory_space=pltpu.VMEM), pl.BlockSpec(memory_space=pltpu.VMEM)),
        scratch_shapes=[
            vmem((widths, candidates), F32),
            vmem((widths, candidates), BF16),
            vmem((widths, candidates), BF16),
            vmem((8, candidates), F32),
            vmem((widths, examples), F32),
            vmem((examples, widths), BF16),
            vmem((examples, widths), BF16),
            vmem((examples, candidates), F32),
            vmem((2, examples, 128), F32),
            vmem((8, 128), F32),
            pltpu.SMEM((2,), jnp.int32),
            vmem((10, 8, 128), F32),
            vmem((LEVELS, 8, 128), F32),
            vmem((widths, 256), BF16),
            vmem((widths, 256), BF16),
            vmem((2, 16, 128), F32),
            vmem((16, 128), F32),
            vmem((LEVELS, 16, 128), F32),
            vmem((2, 16, 128), F32),
            dma((4,)),
            dma((8,)),
            dma((8, 2, PIECES)),
            dma((9,)),
            dma((9,)),
            dma((2, 1)),
            dma((2, 1, 4)),
            dma((2, 4)),
            dma((2, 4, 4)),
            pltpu.SemaphoreType.REGULAR((3, 2)),
            dma((3,)),
            dma((3, 3)),
            dma((2,)),
            dma((2,)),
            dma((2,)),
            dma((2,)),
            dma((4,)),
            dma((4,)),
            dma((4,)),
            dma((4,)),
            dma,
            dma,
        ],
        compiler_params=pltpu.CompilerParams(
            collective_id=0, has_side_effects=True, vmem_limit_bytes=55200 * 1024
        ),
        cost_estimate=pl.CostEstimate(flops=6 * 512 * 1024 * 2048, bytes_accessed=300000, transcendentals=4096),
    )(example_sketch, candidate_sketch, best_start.reshape(8, 128), chosen)
    return jnp.maximum(best.reshape(examples), best_start), gains * (1.0 / 32768.0)


def solution(mesh):
    return jax.shard_map(
        on_device,
        mesh=mesh,
        in_specs=(P("col", "row"), P("row", "col"), P("row"), P()),
        out_specs=(P("row"), P(None, "col")),
        check_vma=False,
    )
```

```python
import functools

import jax
import jax.numpy as jnp
from jax import lax
from jax.experimental import pallas as pl
from jax.experimental.pallas import tpu as pltpu
from jax.sharding import PartitionSpec as P

EPS = 1e-06
LEVELS = 16
GROUP = 32
PIECES = 4
TILE = 256
F32, BF16 = jnp.float32, jnp.bfloat16


def remote(src, dst, send, recv, row, col):
    return pltpu.make_async_remote_copy(
        src_ref=src,
        dst_ref=dst,
        send_sem=send,
        recv_sem=recv,
        device_id={"row": row, "col": col},
        device_id_type=pl.DeviceIdType.MESH,
    )


def slot_rows(slot):
    return pl.ds((slot % LEVELS) * GROUP, GROUP)


def kernel(
    ex_hbm, cand_hbm, best_hbm, chosen_hbm, best_out, gains_out,
    cand, c_hi, c_lo, c_sq, ex, e_hi, e_lo, acc, best_rep, best_in, chosen, ch_part, ch, ch_hi, ch_lo,
    g_own, g_sib, g_all, g_alt, g_sum,
    loc_sem, ring_s, ring_r, sib_s, sib_r, p1_s, p1_r, p2_s, p2_r, wave,
    cx_s, cx_r, z1_s, z1_r, z2_s, z2_r, gs_s, gs_r, gz_s, gz_r, ga_s, ga_r, gf_s, gf_r,
):
    row, col = lax.axis_index("row"), lax.axis_index("col")
    z, c, y, x = row // 2, row % 2, col // 4, col % 4

    def in_x(d):
        return y * 4 + (x + d) % 4

    def in_y(d):
        return ((y + d) % 4) * 4 + x

    def in_z(d):
        return ((z + d + LEVELS) % LEVELS) * 2 + c

    above, below = ((z + 1) % LEVELS) * 2, ((z + LEVELS - 1) % LEVELS) * 2
    sib = z * 2 + 1 - c
    onward = jnp.where(c == 0, above, below + 1)
    sent = []

    def go(*args):
        remote(*args).start()

    def left(view, sem):
        sent.append(remote(view, view, sem, loc_sem.at[0], sib, col))

    def arrived(view, sem):
        remote(view, view, loc_sem.at[0], sem, sib, col).wait_recv()

    barrier = pltpu.get_barrier_semaphore()
    near = [(r, col) for r in (above, above + 1, below, below + 1, sib)]
    near += [(row, t) for d in (1, 2, 3) for t in (in_x(d), in_y(d))]
    for r, t in near:
        pl.semaphore_signal(
            barrier, inc=1, device_id={"row": r, "col": t}, device_id_type=pl.DeviceIdType.MESH
        )

    mine = pl.ds(pl.multiple_of(4 * GROUP + c * 16, 16), 16)

    def ex_view(t, half, rows=16, skip=0):
        slot = (t - z + 4 + LEVELS) % LEVELS
        return ex.at[pl.ds(pl.multiple_of(slot * GROUP + 16 * half + skip, 8), rows)]

    copies = [
        pltpu.make_async_copy(cand_hbm, cand.at[mine], loc_sem.at[0]),
        pltpu.make_async_copy(chosen_hbm, chosen, loc_sem.at[1]),
        pltpu.make_async_copy(ex_hbm, ex_view(col, 0, 32), loc_sem.at[2]),
        pltpu.make_async_copy(best_hbm, best_in, loc_sem.at[3]),
    ]
    for copy in copies:
        copy.start()
    copies[0].wait()
    copies[1].wait()

    lane = lax.broadcasted_iota(jnp.int32, (128, 128), 1)
    sub = lax.broadcasted_iota(jnp.int32, (128, 128), 0)

    block = cand[mine, :]
    wide = lax.broadcasted_iota(jnp.int32, block.shape, 1)
    tile = jnp.zeros((8, 128), F32)
    for r in range(2):
        place = chosen[r] - col * block.shape[1]
        value = jnp.sum(jnp.where(wide == place, block, 0.0), axis=1, keepdims=True)
        line = jnp.sum(
            jnp.where(lane[:16] == sub[:16] + (GROUP * (z % 4) + 16 * c), value, 0.0), axis=0, keepdims=True
        )
        tile = tile + jnp.where(sub[:8] == r, line, 0.0)
    ch_part[0] = tile
    copies[2].wait()
    copies[3].wait()
    pl.semaphore_wait(barrier, len(near))

    def wave_send(i):
        for k, r in enumerate((in_z(1), in_z(-1))):
            pl.semaphore_signal(
                wave.at[i, k], inc=1, device_id={"row": r, "col": col}, device_id_type=pl.DeviceIdType.MESH
            )

    def wave_wait(i):
        pl.semaphore_wait(wave.at[i, 0], 1)
        pl.semaphore_wait(wave.at[i, 1], 1)

    wave_send(0)

    width = cand.shape[1] * 2 // PIECES

    def piece(first_row, half, k):
        start = pl.multiple_of(first_row + 8 * half, 8)
        return cand.at[pl.ds(start, 8), pl.ds((k // 2) * width, width)]

    for k in range(PIECES):
        src = piece(4 * GROUP + c * 16, k % 2, k)
        go(src, piece(3 * GROUP + c * 16, k % 2, k), ring_s.at[0], ring_r.at[0, c, k], above, col)
        go(src, piece(5 * GROUP + c * 16, k % 2, k), ring_s.at[0], ring_r.at[0, c, k], below + 1, col)
    go(cand.at[mine], cand.at[mine], sib_s.at[0], sib_r.at[0], sib, col)
    left(cand.at[pl.ds(0, 32)], ring_s.at[0])
    left(cand.at[pl.ds(0, 16)], sib_s.at[0])
    two = pl.ds(0, 2)
    for j in range(3):
        go(ch_part.at[0, two], ch_part.at[2 + j, two], cx_s.at[0], cx_r.at[0, j], row, in_x(j + 1))
    left(ch.at[pl.ds(0, 3), two], cx_s.at[0])

    lines = ((in_x, in_y), (in_y, in_x))

    def spread(half, phase, i, view):
        s, r = (p1_s, p1_r) if phase == 0 else (p2_s, p2_r)
        for k, d in enumerate((1, 3)):
            go(view, view, s.at[half, i], r.at[half, i, k], row, lines[half][phase](d))
        left(ex.at[pl.ds(0, 48)], s.at[half, i])

    def relay(half, phase, i, k, owner):
        s, r = (p1_s, p1_r) if phase == 0 else (p2_s, p2_r)
        arrived(ex_view(owner, half), r.at[half, i, k])
        view = ex_view(owner, half, 8, 8 * k)
        go(view, view, s.at[half, i], r.at[half, i, 2 + k], row, lines[half][phase]((1, 3)[k]))

    def opposite(half, phase, i):
        r = p1_r if phase == 0 else p2_r
        arrived(ex.at[pl.ds(0, 8)], r.at[half, i, 2])
        arrived(ex.at[pl.ds(0, 8)], r.at[half, i, 3])

    def first(half, d):
        return lines[half][0](d)

    def second(half, d1, d2):
        xx, yy = (d1, d2) if half == 0 else (d2, d1)
        return ((y + yy) % 4) * 4 + (x + xx) % 4

    for half in range(2):
        spread(half, 0, 0, ex_view(col, half))
    for half in range(2):
        spread(half, 1, 0, ex_view(col, half))

    plan = {}

    def at(h, i, *fns):
        i = 7 if 4 < h < 8 else 3 if h == 8 else i
        plan.setdefault((h, i), []).extend(fns)

    def call(fn, *args):
        return functools.partial(fn, *args)

    def phase_one(half, k):
        d = (3, 1)[k]
        relay(half, 0, 0, k, first(half, d))
        spread(half, 1, d, ex_view(first(half, d), half))

    def phase_one_far(half):
        opposite(half, 0, 0)
        spread(half, 1, 2, ex_view(first(half, 2), half))

    def phase_two(half, d, k):
        relay(half, 1, d, k, second(half, d, (3, 1)[k]))

    def from_sib(h):
        arrived(cand.at[pl.ds(0, 16 if h in (0, 8) else GROUP)], sib_r.at[h])

    def prepare(slot):
        v = cand[slot_rows(slot), :]
        hi = v.astype(BF16)
        c_hi[slot_rows(slot), :] = hi
        c_lo[slot_rows(slot), :] = (v - hi.astype(F32)).astype(BF16)
        sq = v * v
        c_sq[...] += sq[0:8] + sq[8:16] + sq[16:24] + sq[24:32]

    def chosen_y():
        for j in range(3):
            arrived(ch_part.at[2 + j, two], cx_r.at[0, j])
        ch_part[1, two] = ch_part[0, two] + ch_part[2, two] + ch_part[3, two] + ch_part[4, two]
        for j in range(3):
            go(ch_part.at[1, two], ch_part.at[5 + j, two], cx_s.at[1], cx_r.at[1, j], row, in_y(j + 1))
        left(ch.at[pl.ds(0, 3), two], cx_s.at[1])

    def chosen_sib():
        for j in range(3):
            arrived(ch_part.at[5 + j, two], cx_r.at[1, j])
        ch_part[8, two] = ch_part[1, two] + ch_part[5, two] + ch_part[6, two] + ch_part[7, two]
        go(ch_part.at[8, two], ch_part.at[9, two], cx_s.at[2], cx_r.at[2, 0], sib, col)
        left(ch.at[0, two], cx_s.at[2])

    def chosen_near():
        arrived(ch_part.at[9, two], cx_r.at[2, 0])
        ch[4, two] = ch_part[8, two] + ch_part[9, two]
        for d in range(1, 5):
            go(ch.at[4, two], ch.at[4 - d, two], z1_s.at[0], z1_r.at[0], in_z(d), col)
            go(ch.at[4, two], ch.at[4 + d, two], z1_s.at[1], z1_r.at[1], in_z(-d), col)
        left(ch.at[pl.ds(0, 4), two], z1_s.at[0])
        left(ch.at[pl.ds(0, 4), two], z1_s.at[1])

    def chosen_far():
        arrived(ch.at[pl.ds(0, 4), two], z1_r.at[0])
        arrived(ch.at[pl.ds(0, 4), two], z1_r.at[1])
        go(ch.at[pl.ds(0, 4), two], ch.at[pl.ds(12, 4), two], z2_s.at[0], z2_r.at[0], in_z(4), col)
        go(ch.at[pl.ds(5, 3), two], ch.at[pl.ds(9, 3), two], z2_s.at[1], z2_r.at[1], in_z(-4), col)
        left(ch.at[pl.ds(0, 4), two], z2_s.at[0])
        left(ch.at[pl.ds(0, 3), two], z2_s.at[1])

    held = {"e_sq": jnp.zeros((8, ex.shape[1]), F32), "ch_sq": [jnp.zeros((1, 128), F32)] * 2}

    def square(part):
        total = held["e_sq"]
        for i in range(32 * part, 32 * part + 32):
            v = ex[pl.ds(8 * i, 8), :]
            total = total + v * v
        held["e_sq"] = total
        if part == 1:
            scale = jnp.sqrt(jnp.float32(LEVELS * GROUP))
            held["factor"] = scale / jnp.sqrt(jnp.sum(total, axis=0, keepdims=True) + EPS)

    def turn(i, q):
        v = ex[pl.ds(128 * q, 128), pl.ds(128 * i, 128)] * held["factor"][:, 128 * i : 128 * (i + 1)]
        v = v.T
        hi = v.astype(BF16)
        e_hi[pl.ds(128 * i, 128), pl.ds(128 * q, 128)] = hi
        e_lo[pl.ds(128 * i, 128), pl.ds(128 * q, 128)] = (v - hi.astype(F32)).astype(BF16)

    def chosen_wide(q):
        four = ch[4 * q, two] + ch[4 * q + 1, two] + ch[4 * q + 2, two] + ch[4 * q + 3, two]
        for r in range(2):
            v = jnp.broadcast_to(four[r : r + 1, :], (128, 128)).T
            held["ch_sq"] = [
                s + jnp.sum(v * v, axis=0, keepdims=True) if k == r else s for k, s in enumerate(held["ch_sq"])
            ]
            hi = v.astype(BF16)
            lo = (v - hi.astype(F32)).astype(BF16)
            for b in range(4):
                to = pl.ds(pl.multiple_of(((b - z + LEVELS) % 4 + 4 * q) * GROUP, GROUP), GROUP)
                ch_hi[to, pl.ds(128 * r, 128)] = hi[32 * b : 32 * b + 32]
                ch_lo[to, pl.ds(128 * r, 128)] = lo[32 * b : 32 * b + 32]

    def chosen_come():
        arrived(ch.at[pl.ds(0, 4), two], z2_r.at[0])
        arrived(ch.at[pl.ds(0, 3), two], z2_r.at[1])

    dot = functools.partial(jnp.dot, preferred_element_type=F32)

    def pick(i):
        rows = pl.ds(i * 256, 256)
        hi, lo = e_hi[rows, :], e_lo[rows, :]
        d = dot(hi, ch_hi[...]) + dot(lo, ch_hi[...]) + dot(hi, ch_lo[...])
        b = best_rep[0, rows, :]
        for r in range(2):
            b = jnp.maximum(b, d[:, 128 * r : 128 * r + 128] / jnp.sqrt(held["ch_sq"][r] + EPS))
            best_rep[r, rows, :] = b
        for k in range(2):
            best_out[pl.ds(2 * i + k, 1), :] = jnp.sum(
                jnp.where(lane == sub, b[128 * k : 128 * k + 128], 0.0), axis=0, keepdims=True
            )

    def first_half(n, m):
        cols, rows = pl.ds(n * TILE, TILE), pl.ds(m * 512, 512)
        hi, lo = c_hi[pl.ds(0, 256), cols], c_lo[pl.ds(0, 256), cols]
        a_hi, a_lo = e_hi[rows, pl.ds(0, 256)], e_lo[rows, pl.ds(0, 256)]
        acc[rows, cols] = dot(a_hi, hi) + dot(a_lo, hi) + dot(a_hi, lo)

    at(1, 3, call(wave_wait, 2), chosen_y)
    at(2, 7, chosen_sib)
    at(3, 3, chosen_near)
    at(5, 4, chosen_far)
    at(7, 2, chosen_come, call(chosen_wide, 0))
    at(7, 3, call(chosen_wide, 1))
    at(7, 4, call(chosen_wide, 2))
    at(7, 5, call(chosen_wide, 3))
    for n, (half, k) in enumerate(((0, 0), (0, 1), (1, 0), (1, 1))):
        at(1, (1, 2, 4, 5)[n], call(phase_one, half, k))
        at(2, n, call(phase_two, half, 0, k))
        at(3, 2 * (n % 2) + 1, call(phase_two, half, 1, k))
        at(3, 2 * (n % 2) + 4, call(phase_two, half, 3, k))
        at(4, n, call(phase_two, half, 2, k))
    at(2, 5, call(phase_one_far, 0))
    at(2, 6, call(phase_one_far, 1))
    for half in range(2):
        for d in range(4):
            at(5, 0, call(opposite, half, 1, d))
    at(5, 1, call(square, 0))
    at(5, 2, call(square, 1))
    work = [call(turn, i, q) for q in range(2) for i in range(8)]
    for i, fn in enumerate(work):
        at(5, 3 + i // 4, fn)
    work = [call(turn, i, q) for q in range(2, 4) for i in range(8)]
    for i, fn in enumerate(work):
        at(6, 6 + i // 8, fn)
    for h in range(1, 7):
        at(h + 1, 3, call(from_sib, h))
        at(h + 1, 4, call(prepare, (4 - h) % LEVELS))
        at(h + 1, 5, call(prepare, 4 + h))
    halves = [(n, m) for n in range(8) for m in range(2)]
    for i, (n, m) in enumerate(halves[:3]):
        at(6, i, call(first_half, n, m))
    for i, (n, m) in enumerate(halves[3:8]):
        at(7, i, call(first_half, n, m))
    for i, (n, m) in enumerate(halves[8:]):
        at(8, 3, call(first_half, n, m))
    for i in range(4):
        at(7, 6 + i // 2, call(pick, i))

    c_sq[...] = jnp.zeros_like(c_sq)
    for i in range(8):
        best_rep[0, pl.ds(128 * i, 128), :] = jnp.broadcast_to(best_in[pl.ds(i, 1), :], (128, 128)).T
    wave_wait(0)
    wave_send(1)
    from_sib(0)
    prepare(4)
    wave_wait(1)
    wave_send(2)

    for h in range(1, 9):
        base = jnp.where(c == 0, ((4 - h) % LEVELS) * GROUP, ((4 + h) % LEVELS) * GROUP)
        after = jnp.where(c == 0, ((3 - h) % LEVELS) * GROUP, ((5 + h) % LEVELS) * GROUP)
        event = 0
        for k in range(PIECES):
            for o in range(2):
                far = k % 2 == 0
                if h == 8 and not far:
                    continue
                half = (k % 2 + c) % 2
                view = piece(base + o * 16, half, k)
                kk = (k // 2) * 2 + half if h == 1 else k
                arrived(view, ring_r.at[h - 1, o, kk])
                if h < 7 or (far and h < 8):
                    go(view, piece(after + o * 16, half, k), ring_s.at[h], ring_r.at[h, o, k], onward, col)
                go(view, view, sib_s.at[h], sib_r.at[h], sib, col)
                for fn in plan.pop((h, event), ()):
                    fn()
                event += 1
        if h < 8:
            left(cand.at[pl.ds(0, 32 if h < 7 else 16)], ring_s.at[h])
        left(cand.at[pl.ds(0, 32 if h < 8 else 16)], sib_s.at[h])
    assert not plan
    from_sib(7)
    prepare(13)
    prepare(11)
    from_sib(8)
    prepare(12)

    def second_half(n, _):
        cols = pl.ds(pl.multiple_of(n * TILE, TILE), TILE)
        hi, lo = c_hi[pl.ds(256, 256), cols], c_lo[pl.ds(256, 256), cols]
        a_hi, a_lo = e_hi[:, pl.ds(256, 256)], e_lo[:, pl.ds(256, 256)]
        d = acc[:, cols] + (dot(a_hi, hi) + dot(a_lo, hi) + dot(a_hi, lo))
        norm = jnp.sqrt(jnp.sum(c_sq[:, cols], axis=0, keepdims=True) + EPS)
        sim = d * (1.0 / norm)
        for r in range(2):
            b = best_rep[r]
            for t in range(2):
                part = jnp.maximum(sim[:, 128 * t : 128 * t + 128] - b, 0.0)
                g_own[r, pl.ds(2 * n + t, 1), :] = jnp.sum(part, axis=0, keepdims=True)
        return 0

    def rows_of(p):
        return pl.ds(4 * p, 4)

    def to_sib(p):
        go(g_own.at[1 - c, rows_of(p)], g_sib.at[rows_of(p)], gs_s.at[p], gs_r.at[p], sib, col)
        left(g_sib.at[rows_of(p)], gs_s.at[p])

    def to_levels(p):
        part = rows_of(p)
        arrived(g_sib.at[part], gs_r.at[p])
        g_all[0, part] = g_own[c, part] + g_sib[part]
        for d in (8, 7, 9, 6, 10, 5, 11, 4, 12, 3, 13, 2, 14, 1, 15):
            go(g_all.at[0, part], g_all.at[d, part], gz_s.at[p], gz_r.at[p], in_z(d), col)
            if p == 3:
                go(g_all.at[0, part], g_alt.at[d], ga_s, ga_r, in_z(d) + 1 - 2 * c, col)
        left(g_all.at[pl.ds(1, 15), part], gz_s.at[p])
        if p == 3:
            go(g_all.at[0, part], g_alt.at[0], ga_s, ga_r, sib, col)
            left(g_alt, ga_s)

    for p in range(4):
        lax.fori_loop(2 * p, 2 * p + 2, second_half, 0)
        to_sib(p)
        if p > 0:
            to_levels(p - 1)
    to_levels(3)
    for copy in sent:
        copy.wait_send()
    for p in range(3):
        arrived(g_all.at[pl.ds(1, 15), rows_of(p)], gz_r.at[p])
    early = pl.ds(0, 12)
    total = g_all[0, early]
    for d in range(1, LEVELS):
        total = total + g_all[d, early]
    g_sum[c, early] = total
    go(g_sum.at[c, early], g_sum.at[c, early], gf_s, gf_r, sib, col)
    arrived(g_sum.at[1 - c, early], gf_r)
    remote(g_sum.at[c, early], g_sum.at[c, early], gf_s, gf_r, sib, col).wait_send()
    last = rows_of(3)
    arrived(g_all.at[pl.ds(1, 15), last], gz_r.at[3])
    arrived(g_alt, ga_r)
    total, other = g_all[0, last], g_alt[0]
    for d in range(1, LEVELS):
        total, other = total + g_all[d, last], other + g_alt[d]
    g_sum[c, last] = total
    g_sum[1 - c, last] = other
    for r in range(2):
        for t in range(16):
            gains_out[pl.ds(r, 1), pl.ds(128 * t, 128)] = g_sum[r, pl.ds(t, 1), :]


def on_device(example_sketch, candidate_sketch, best_start, chosen):
    dma = pltpu.SemaphoreType.DMA
    vmem = pltpu.VMEM
    examples, candidates = example_sketch.shape[1], candidate_sketch.shape[1]
    widths = LEVELS * GROUP
    best, gains = pl.pallas_call(
        kernel,
        out_shape=(
            jax.ShapeDtypeStruct((8, 128), F32),
            jax.ShapeDtypeStruct((2, candidates), F32),
        ),
        in_specs=[
            pl.BlockSpec(memory_space=pltpu.HBM),
            pl.BlockSpec(memory_space=pltpu.HBM),
            pl.BlockSpec(memory_space=pltpu.HBM),
            pl.BlockSpec(memory_space=pltpu.HBM),
        ],
        out_specs=(pl.BlockSpec(memory_space=pltpu.VMEM), pl.BlockSpec(memory_space=pltpu.VMEM)),
        scratch_shapes=[
            vmem((widths, candidates), F32),
            vmem((widths, candidates), BF16),
            vmem((widths, candidates), BF16),
            vmem((8, candidates), F32),
            vmem((widths, examples), F32),
            vmem((examples, widths), BF16),
            vmem((examples, widths), BF16),
            vmem((examples, candidates), F32),
            vmem((2, examples, 128), F32),
            vmem((8, 128), F32),
            pltpu.SMEM((2,), jnp.int32),
            vmem((10, 8, 128), F32),
            vmem((LEVELS, 8, 128), F32),
            vmem((widths, 256), BF16),
            vmem((widths, 256), BF16),
            vmem((2, 16, 128), F32),
            vmem((16, 128), F32),
            vmem((LEVELS, 16, 128), F32),
            vmem((LEVELS, 4, 128), F32),
            vmem((2, 16, 128), F32),
            dma((4,)),
            dma((8,)),
            dma((8, 2, PIECES)),
            dma((9,)),
            dma((9,)),
            dma((2, 1)),
            dma((2, 1, 4)),
            dma((2, 4)),
            dma((2, 4, 4)),
            pltpu.SemaphoreType.REGULAR((3, 2)),
            dma((3,)),
            dma((3, 3)),
            dma((2,)),
            dma((2,)),
            dma((2,)),
            dma((2,)),
            dma((4,)),
            dma((4,)),
            dma((4,)),
            dma((4,)),
            dma,
            dma,
            dma,
            dma,
        ],
        compiler_params=pltpu.CompilerParams(
            collective_id=0, has_side_effects=True, vmem_limit_bytes=55200 * 1024
        ),
        cost_estimate=pl.CostEstimate(flops=6 * 512 * 1024 * 2048, bytes_accessed=300000, transcendentals=4096),
    )(example_sketch, candidate_sketch, best_start.reshape(8, 128), chosen)
    return jnp.maximum(best.reshape(examples), best_start), gains * (1.0 / 32768.0)


def solution(mesh):
    return jax.shard_map(
        on_device,
        mesh=mesh,
        in_specs=(P("col", "row"), P("row", "col"), P("row"), P()),
        out_specs=(P("row"), P(None, "col")),
        check_vma=False,
    )
```
